128 devices in a mesh: group: 16 (over x_lo, z, core), inner: 8 (over y, x_hi).
Axes of the slice: x: 4 (x_hi: 2, x_lo: 2; x = x_hi * 2 + x_lo), y: 4, z: 4, core: 2. Of those that a mesh axis runs over, the one named last changes fastest.
Arguments:
- clips: bfloat16 [16384, 8, 1152], P(('group', 'inner')), may hold values from -6 to 6
- counts: int32 [16384], P(('group', 'inner')), may hold values from 1 to 8
- texts: bfloat16 [16384, 1152], P(('group', 'inner')), may hold values from -6 to 6
- log_scale: float32 [1], replicated, may hold values from 2 to 3
- bias: float32 [1], replicated, may hold values from -3 to -1
Outputs:
- clip_grad: float32 [16384, 8, 1152], P(('group', 'inner'))
- text_grad: float32 [16384, 1152], P(('group', 'inner'))
The draws below stay inside these ranges and needn't reach their ends.
Inputs may be any that keep to these rules, and one draw needn't show every extreme that they name: `counts`: slots at and beyond a video's count are ignored.
All inputs are finite; a program needn't handle non-finite values.
Results may differ from the reference program's by a relative error of at most 0.0048.
Values may be sent and summed in bfloat16 or wider, within the bound.
A program may use at most 256 MiB of HBM per device.

```python
import jax
import jax.numpy as jnp
from jax import lax

D = 1152
SLOTS = 8
VIDEOS = 16384


def with_ends(entries, own_key, low, largest):
    dims = entries.shape
    place = [jax.random.randint(jax.random.fold_in(own_key, axis), (), 0, dims[axis]) for axis in range(len(dims))]
    entries = entries.at[tuple(place)].set(low)
    longest = dims.index(max(dims))
    place[longest] = (place[longest] + 1) % dims[longest]
    return entries.at[tuple(place)].set(largest)


def block_levels(rng, dims, pieces, least, largest):
    level, own = 1.0, jax.random.fold_in(rng, 6)
    for position, blocks in pieces:
        steps = jnp.exp(jax.random.uniform(jax.random.fold_in(own, position), (blocks,), jnp.float32, least / len(pieces), largest / len(pieces)))
        level = level * jnp.repeat(steps, dims[position] // blocks).reshape([-1 if axis == position else 1 for axis in range(len(dims))])
    return level


def scatter_about(key, dims, deviation, reach, split=(), kind=jnp.bfloat16):
    values = deviation * jax.random.normal(key, dims, jnp.float32)
    if split:
        values = values * block_levels(key, dims, split, -0.22, 0.18)
    return jnp.clip(values, -reach, reach).astype(kind)


def setup_inputs(seed: int = 0) -> dict:
    keys = jax.random.split(jax.random.key(seed), 6)
    clips = scatter_about(keys[0], (VIDEOS, SLOTS, D), 1.0, 6.0, ((0, 128),))
    counts = with_ends(jax.random.randint(keys[1], (VIDEOS,), 1, 9), jax.random.fold_in(keys[1], 1), 1, 8).astype(jnp.int32)
    texts = scatter_about(keys[2], (VIDEOS, D), 1.0, 6.0, ((0, 128),))
    log_scale = jnp.clip(jax.random.uniform(keys[3], (1,), jnp.float32, 2.0, 3.0), 2.0, 3.0)
    bias = jnp.clip(jax.random.uniform(keys[4], (1,), jnp.float32, -3.0, -1.0), -3.0, -1.0)
    return {"clips": clips, "counts": counts, "texts": texts, "log_scale": log_scale, "bias": bias}


def reference(clips, counts, texts, log_scale, bias):
    eps = 1e-06
    slot_ids = jnp.arange(SLOTS, dtype=jnp.int32)
    used = (slot_ids[None, :] < counts[:, None]).astype(jnp.float32)
    count_f = counts.astype(jnp.float32)
    pooled = lax.optimization_barrier(jnp.sum(clips.astype(jnp.float32) * used[:, :, None], axis=1)) / count_f[:, None]
    vid_norm = jnp.sqrt(lax.optimization_barrier(jnp.sum(pooled * pooled, axis=1, keepdims=True)) + eps)
    vid_unit = pooled / vid_norm
    vid_half = vid_unit.astype(jnp.bfloat16)
    text_f = texts.astype(jnp.float32)
    txt_norm = jnp.sqrt(lax.optimization_barrier(jnp.sum(text_f * text_f, axis=1, keepdims=True)) + eps)
    txt_unit = text_f / txt_norm
    txt_half = txt_unit.astype(jnp.bfloat16)
    scale = jnp.exp(log_scale[0])
    logits = scale * jnp.dot(vid_half, txt_half.T, preferred_element_type=jnp.float32) + bias[0]
    eye = jnp.eye(VIDEOS, dtype=jnp.float32)
    coef = (jax.nn.sigmoid(logits) - eye).astype(jnp.bfloat16)
    vid_back = scale * jnp.dot(coef, txt_half, preferred_element_type=jnp.float32)
    txt_back = scale * jnp.dot(coef.T, vid_half, preferred_element_type=jnp.float32)
    text_grad = (txt_back - txt_unit * lax.optimization_barrier(jnp.sum(txt_unit * txt_back, axis=1, keepdims=True))) / txt_norm
    pool_back = (vid_back - vid_unit * lax.optimization_barrier(jnp.sum(vid_unit * vid_back, axis=1, keepdims=True))) / vid_norm
    clip_grad = (pool_back / count_f[:, None])[:, None, :] * used[:, :, None]
    return (clip_grad, text_grad)
```

```python
import functools

import jax
import jax.numpy as jnp
from jax import lax
from jax.experimental import pallas as pl
from jax.experimental.pallas import tpu as pltpu
from jax.sharding import PartitionSpec as P

MESH = pl.DeviceIdType.MESH
ROWS = 128
HALF = ROWS // 2
PAIR = 2 * ROWS
SLOTS = 8
BLOCKS = 8
EPS = 1e-06

OWN, MATE, UP, DOWN, MATE_UP, MATE_DOWN, FAR, MATE_FAR = range(BLOCKS)


def device_at(x, y, z, core):
    return ((x % 2) * 8 + z * 2 + core, y * 2 + x // 2)


class Places:
    def __init__(self):
        group, inner = lax.axis_index("group"), lax.axis_index("inner")
        core, z, y = group % 2, (group // 2) % 4, inner // 2
        x = (inner % 2) * 2 + group // 8
        odd = x % 2
        self.sibling = device_at(x, y, z, 1 - core)
        self.vid = (
            device_at(x + 1 - 2 * odd, y, z, core),
            device_at(x, (y + 1) % 4, z, core),
            device_at(x, (y + 3) % 4, z, core),
        )
        self.txt = (
            device_at((x + 3 + 2 * odd) % 4, y, z, core),
            device_at(x, y, (z + 1) % 4, core),
            device_at(x, y, (z + 3) % 4, core),
        )

    def all(self):
        return (self.sibling, *self.vid, *self.txt)


GATHER = (
    (0, OWN, MATE, 0),
    (0, OWN, MATE, 1),
    (1, OWN, DOWN, 0),
    (1, OWN, DOWN, 1),
    (2, OWN, UP, 0),
    (2, OWN, UP, 1),
    (1, DOWN, FAR, 0),
    (2, UP, FAR, 1),
    (1, MATE, MATE_DOWN, 0),
    (1, MATE, MATE_DOWN, 1),
    (2, MATE, MATE_UP, 0),
    (2, MATE, MATE_UP, 1),
    (0, FAR, MATE_FAR, 0),
    (0, FAR, MATE_FAR, 1),
)
REDUCE = (
    (0, MATE_FAR, 0),
    (0, MATE_FAR, 1),
    (1, MATE_UP, 0),
    (1, MATE_UP, 1),
    (2, MATE_DOWN, 0),
    (2, MATE_DOWN, 1),
    (2, FAR, 0),
    (1, FAR, 1),
    (0, MATE, 0),
    (0, MATE, 1),
    (1, UP, 0),
    (1, UP, 1),
    (2, DOWN, 0),
    (2, DOWN, 1),
)


class Side:
    def __init__(self, near, blocks, stride, terms, stage, landed, gather_sems, reduce_sems):
        self.near, self.blocks, self.stride = near, blocks, stride
        self.terms, self.stage, self.landed = terms, stage, landed
        self.gather_sems, self.reduce_sems = gather_sems, reduce_sems

    def rows(self, block, half):
        return self.blocks.at[pl.ds(block * self.stride + half * HALF, HALF)]

    def gather(self, i):
        to, source, target, half = GATHER[i]
        return pltpu.make_async_remote_copy(
            src_ref=self.rows(source, half),
            dst_ref=self.rows(target, half),
            send_sem=self.gather_sems.at[0, i],
            recv_sem=self.gather_sems.at[1, i],
            device_id=self.near[to],
            device_id_type=MESH,
        )

    def send(self, *ids):
        for i in ids:
            self.gather(i).start()

    def take(self, *ids):
        for i in ids:
            self.gather(i).wait_recv()

    def reduce(self, i):
        return pltpu.make_async_remote_copy(
            src_ref=self.stage.at[i],
            dst_ref=self.landed.at[i],
            send_sem=self.reduce_sems.at[0, i],
            recv_sem=self.reduce_sems.at[1, i],
            device_id=self.near[REDUCE[i][0]],
            device_id_type=MESH,
        )

    def part(self, block, half):
        return self.terms[pl.ds(block * ROWS + half * HALF, HALF)]

    def give(self, i, *arrived):
        _, block, half = REDUCE[i]
        total = self.part(block, half)
        for j in arrived:
            self.reduce(j).wait_recv()
            total = total + self.landed[j].astype(jnp.float32)
        self.stage[i] = total.astype(jnp.bfloat16)
        self.reduce(i).start()

    def finish(self):
        for i in range(len(GATHER)):
            self.gather(i).wait_send()
        for i in range(len(REDUCE)):
            self.reduce(i).wait_send()


def kernel(
    log_scale_ref, bias_ref, counts_ref, texts_hbm, clips_hbm,
    pool_ref, text_ref,
    texts, clips, vids, txts, coef,
    vid_unit, vid_norm, count_col, txt_unit, txt_norm,
    vid_terms, txt_terms, vid_stage, vid_landed, txt_stage, txt_landed, sib_stage, sib_landed,
    load_sems, vid_gather, vid_reduce, txt_gather, txt_reduce, sib_gather, sib_reduce,
):
    places = Places()
    barrier = pltpu.get_barrier_semaphore()
    for near in places.all():
        pl.semaphore_signal(barrier, inc=1, device_id=near, device_id_type=MESH)
    load_texts = pltpu.make_async_copy(texts_hbm, texts, load_sems.at[0])
    load_clips = pltpu.make_async_copy(clips_hbm, clips, load_sems.at[1])
    load_texts.start()
    load_clips.start()

    vid = Side(places.vid, vids, ROWS, vid_terms, vid_stage, vid_landed, vid_gather, vid_reduce)
    txt = Side(places.txt, txts, PAIR, txt_terms, txt_stage, txt_landed, txt_gather, txt_reduce)

    def to_sibling(block):
        return pltpu.make_async_remote_copy(
            src_ref=txts.at[pl.ds(block * PAIR, ROWS)],
            dst_ref=txts.at[pl.ds(block * PAIR + ROWS, ROWS)],
            send_sem=sib_gather.at[0, block],
            recv_sem=sib_gather.at[1, block],
            device_id=places.sibling,
            device_id_type=MESH,
        )

    def terms_to_sibling(block):
        return pltpu.make_async_remote_copy(
            src_ref=sib_stage.at[block],
            dst_ref=sib_landed.at[block],
            send_sem=sib_reduce.at[0, block],
            recv_sem=sib_reduce.at[1, block],
            device_id=places.sibling,
            device_id_type=MESH,
        )

    scale = jnp.exp(jnp.full((1, 1), log_scale_ref[0], jnp.float32))
    bias = bias_ref[0]

    load_texts.wait()
    text_f = texts[...].astype(jnp.float32)
    norm = jnp.sqrt(jnp.sum(text_f * text_f, axis=1, keepdims=True) + EPS)
    unit = text_f / norm
    txt_unit[...] = unit
    txt_norm[...] = norm
    txts[pl.ds(0, ROWS)] = unit.astype(jnp.bfloat16)

    pl.semaphore_wait(barrier, len(places.all()))
    txt.send(2, 5, 0)
    to_sibling(OWN).start()
    txt.send(3, 4, 1)

    wide = jnp.broadcast_to(counts_ref[...].astype(jnp.float32), (ROWS, ROWS))
    column = jnp.transpose(wide)[:, 0:1]
    count_col[...] = column
    shape = (ROWS, ROWS * SLOTS)
    slot = lax.broadcasted_iota(jnp.int32, shape, 1)
    video = lax.broadcasted_iota(jnp.int32, shape, 0)
    slot = slot - video * SLOTS
    used = jnp.logical_and(slot >= 0, slot.astype(jnp.float32) < column)
    load_clips.wait()
    pooled = jnp.dot(
        used.astype(jnp.float32).astype(jnp.bfloat16), clips[...], preferred_element_type=jnp.float32
    ) / column
    norm = jnp.sqrt(jnp.sum(pooled * pooled, axis=1, keepdims=True) + EPS)
    unit = pooled / norm
    vid_unit[...] = unit
    vid_norm[...] = norm
    vids[pl.ds(0, ROWS)] = unit.astype(jnp.bfloat16)
    vid.send(2, 5, 0, 3, 4, 1)

    def coefs(first, count, block, own=False):
        columns = pl.ds(pl.multiple_of(block * PAIR, PAIR), PAIR)
        dots = lax.dot_general(
            vids[pl.ds(first * ROWS, count * ROWS)],
            txts[columns],
            (((1,), (1,)), ((), ())),
            preferred_element_type=jnp.float32,
        )
        logits = scale * dots + bias
        values = 1.0 / (1.0 + jnp.exp(-logits))
        if own:
            row = lax.broadcasted_iota(jnp.int32, values.shape, 0)
            col = lax.broadcasted_iota(jnp.int32, values.shape, 1)
            values = values - (row == col).astype(jnp.float32)
        coef[pl.ds(first * ROWS, count * ROWS), columns] = values.astype(jnp.bfloat16)

    def coefs_over(first, count, start, stop):
        @pl.loop(start, stop)
        def _(block):
            coefs(first, count, block)

    to_sibling(OWN).wait_recv()
    coefs(0, 1, OWN, own=True)

    for side in (txt, vid):
        side.take(2)
        side.send(6)
        side.take(5)
        side.send(7)
        side.take(0)
        side.send(8, 10)
    for side in (txt, vid):
        side.take(1)
        side.send(9, 11)
    txt.take(3, 4)
    for block in (MATE, UP, DOWN):
        to_sibling(block).start()
    vid.take(3, 4)
    coefs(1, 3, OWN)
    for block in (MATE, UP, DOWN):
        to_sibling(block).wait_recv()
    coefs_over(0, 4, MATE, DOWN)
    for side in (txt, vid):
        side.take(6)
        side.send(12)
        side.take(7)
        side.send(13)
    to_sibling(FAR).start()
    coefs(0, 4, DOWN)
    coefs_over(FAR, 1, OWN, MATE_UP)
    to_sibling(FAR).wait_recv()
    coefs(0, 4, FAR)
    coefs(FAR, 1, FAR)
    txt.take(8, 9, 10, 11)
    to_sibling(MATE_UP).start()
    to_sibling(MATE_DOWN).start()
    vid.take(8, 9, 10, 11)
    coefs_over(MATE_UP, 2, OWN, MATE_UP)
    coefs(MATE_UP, 2, FAR)
    to_sibling(MATE_UP).wait_recv()
    to_sibling(MATE_DOWN).wait_recv()
    coefs_over(0, 7, MATE_UP, FAR)
    txt.take(12, 13)
    to_sibling(MATE_FAR).start()
    vid.take(12, 13)
    coefs_over(MATE_FAR, 1, OWN, MATE_FAR)
    to_sibling(MATE_FAR).wait_recv()
    coefs(0, 8, MATE_FAR)

    def vid_back(first):
        vid_terms[pl.ds(first * ROWS, PAIR)] = jnp.dot(
            coef[pl.ds(first * ROWS, PAIR)], txts[...], preferred_element_type=jnp.float32
        )

    def txt_back(block):
        terms = lax.dot_general(
            coef[:, pl.ds(block * PAIR, PAIR)],
            vids[...],
            (((0,), (0,)), ((), ())),
            preferred_element_type=jnp.float32,
        )
        txt_terms[pl.ds(block * ROWS, ROWS)] = terms[:ROWS]
        sib_stage[block] = terms[ROWS:].astype(jnp.bfloat16)
        terms_to_sibling(block).start()

    def join(block):
        terms_to_sibling(block).wait_recv()
        here = pl.ds(block * ROWS, ROWS)
        txt_terms[here] = txt_terms[here] + sib_landed[block].astype(jnp.float32)

    vid_back(FAR)
    vid.give(0)
    vid.give(1)
    txt_back(MATE_FAR)
    vid_back(MATE_UP)
    for i in (2, 4, 3, 5):
        vid.give(i)
    txt_back(MATE_UP)
    join(MATE_FAR)
    txt.give(0)
    txt.give(1)
    txt_back(MATE_DOWN)
    join(MATE_UP)
    txt.give(2)
    txt.give(3)
    txt_back(FAR)
    join(MATE_DOWN)
    txt.give(4)
    txt.give(5)
    vid_back(OWN)
    vid.give(6, 0)
    vid.give(7, 1)
    vid_back(UP)
    vid.give(10)
    vid.give(13)
    txt_back(MATE)
    join(FAR)
    txt.give(6, 0)
    txt.give(7, 1)
    vid.give(8, 2, 4)
    vid.give(9, 3, 5)
    txt_back(UP)
    vid.give(12, 6)
    vid.give(11, 7)
    txt_back(DOWN)
    join(MATE)
    txt.give(8, 2, 4)
    txt.give(9, 3, 5)
    join(UP)
    txt.give(10)
    join(DOWN)
    txt.give(13)
    txt_back(OWN)
    txt.give(12, 6)
    txt.give(11, 7)

    def total(side, messages):
        for i in messages:
            side.reduce(i).wait_recv()
        top, bottom = (
            side.part(OWN, half)
            + side.landed[8 + half].astype(jnp.float32)
            + side.landed[10 + half].astype(jnp.float32)
            + side.landed[12 + half].astype(jnp.float32)
            for half in (0, 1)
        )
        return scale * jnp.concatenate([top, bottom], axis=0)

    back = total(vid, range(8, 14))
    unit = vid_unit[...]
    back = (back - unit * jnp.sum(unit * back, axis=1, keepdims=True)) / vid_norm[...]
    pool_ref[...] = back / count_col[...]
    join(OWN)
    back = total(txt, range(8, 14))
    unit = txt_unit[...]
    text_ref[...] = (back - unit * jnp.sum(unit * back, axis=1, keepdims=True)) / txt_norm[...]

    vid.finish()
    txt.finish()
    for block in range(BLOCKS):
        to_sibling(block).wait_send()
        terms_to_sibling(block).wait_send()


def on_device(clips, counts, texts, log_scale, bias):
    videos, slots, width = clips.shape
    bf16, f32 = jnp.bfloat16, jnp.float32
    smem = pl.BlockSpec(memory_space=pltpu.SMEM)
    vmem = pl.BlockSpec(memory_space=pltpu.VMEM)
    hbm = pl.BlockSpec(memory_space=pl.ANY)
    dma = pltpu.SemaphoreType.DMA
    own = jax.ShapeDtypeStruct((videos, width), f32)
    pool_grad, text_grad = pl.pallas_call(
        kernel,
        out_shape=(own, own),
        in_specs=[smem, smem, vmem, hbm, hbm],
        out_specs=(vmem, vmem),
        scratch_shapes=[
            pltpu.VMEM((ROWS, width), bf16),
            pltpu.VMEM((ROWS * SLOTS, width), bf16),
            pltpu.VMEM((BLOCKS * ROWS, width), bf16),
            pltpu.VMEM((BLOCKS * PAIR, width), bf16),
            pltpu.VMEM((BLOCKS * ROWS, BLOCKS * PAIR), bf16),
            pltpu.VMEM((ROWS, width), f32),
            pltpu.VMEM((ROWS, 1), f32),
            pltpu.VMEM((ROWS, 1), f32),
            pltpu.VMEM((ROWS, width), f32),
            pltpu.VMEM((ROWS, 1), f32),
            pltpu.VMEM((BLOCKS * ROWS, width), f32),
            pltpu.VMEM((BLOCKS * ROWS, width), f32),
            pltpu.VMEM((len(REDUCE), HALF, width), bf16),
            pltpu.VMEM((len(REDUCE), HALF, width), bf16),
            pltpu.VMEM((len(REDUCE), HALF, width), bf16),
            pltpu.VMEM((len(REDUCE), HALF, width), bf16),
            pltpu.VMEM((BLOCKS, ROWS, width), bf16),
            pltpu.VMEM((BLOCKS, ROWS, width), bf16),
            dma((2,)),
            dma((2, len(GATHER))),
            dma((2, len(REDUCE))),
            dma((2, len(GATHER))),
            dma((2, len(REDUCE))),
            dma((2, BLOCKS)),
            dma((2, BLOCKS)),
        ],
        compiler_params=pltpu.CompilerParams(
            collective_id=0, has_side_effects=True, vmem_limit_bytes=60 * 1024 * 1024
        ),
        cost_estimate=pl.CostEstimate(
            flops=6 * 1024 * 2048 * width, bytes_accessed=4 * 1024 * 1024, transcendentals=2 * 1024 * 2048
        ),
    )(log_scale, bias, counts.reshape(1, videos), texts, clips.reshape(videos * slots, width))
    slot_ids = lax.broadcasted_iota(jnp.int32, (videos, slots), 1)
    used = (slot_ids < counts[:, None]).astype(f32)
    return pool_grad[:, None, :] * used[:, :, None], text_grad


def solution(mesh):
    return jax.shard_map(
        on_device,
        mesh=mesh,
        in_specs=(
            P(("group", "inner"), None, None),
            P(("group", "inner")),
            P(("group", "inner"), None),
            P(),
            P(),
        ),
        out_specs=(P(("group", "inner"), None, None), P(("group", "inner"), None)),
        check_vma=False,
    )
```

```python
import functools

import jax
import jax.numpy as jnp
from jax import lax
from jax.experimental import pallas as pl
from jax.experimental.pallas import tpu as pltpu
from jax.sharding import PartitionSpec as P

MESH = pl.DeviceIdType.MESH
ROWS = 128
SLOTS = 8
BLOCKS = 8
EPS = 1e-06

OWN, MATE, UP, DOWN, FAR = ((i * ROWS, ROWS) for i in range(5))
MATE_UP = ((640, 64), (768, 64))
MATE_DOWN = ((704, 64), (832, 64))
MATE_FAR = (896, ROWS)
PIECES = (OWN, MATE, UP, DOWN, FAR, MATE_UP[0], MATE_DOWN[0], MATE_UP[1], MATE_DOWN[1], MATE_FAR)
EARLY, MIDDLE, ALL = 640, 768, 1024


def device_at(x, y, z, core):
    return ((x % 2) * 8 + z * 2 + core, y * 2 + x // 2)


class Places:
    def __init__(self):
        group, inner = lax.axis_index("group"), lax.axis_index("inner")
        core, z, y = group % 2, (group // 2) % 4, inner // 2
        x = (inner % 2) * 2 + group // 8
        odd = x % 2
        self.sibling = device_at(x, y, z, 1 - core)
        self.vid = (
            device_at(x + 1 - 2 * odd, y, z, core),
            device_at(x, (y + 1) % 4, z, core),
            device_at(x, (y + 3) % 4, z, core),
        )
        self.txt = (
            device_at((x + 3 + 2 * odd) % 4, y, z, core),
            device_at(x, y, (z + 1) % 4, core),
            device_at(x, y, (z + 3) % 4, core),
        )

    def all(self):
        return (self.sibling, *self.vid, *self.txt)


GATHER = (
    *((1, OWN, DOWN, row, rows) for row, rows in ((0, 32), (32, 32), (64, 64))),
    *((2, OWN, UP, row, rows) for row, rows in ((64, 32), (96, 32), (0, 64))),
    *((0, OWN, MATE, row, 64) for row in (0, 64)),
    *((1, DOWN, FAR, row, 32) for row in (0, 32)),
    *((2, UP, FAR, row, 32) for row in (64, 96)),
    *((1, MATE, MATE_DOWN, row, 64) for row in (0, 64)),
    *((2, MATE, MATE_UP, row, 64) for row in (0, 64)),
    *((0, FAR, MATE_FAR, row, 32) for row in (0, 64, 32, 96)),
)
REDUCE = (
    *((0, MATE_FAR, row, 32) for row in (0, 64, 32, 96)),
    *((1, MATE_UP[half], 0, 64) for half in (0, 1)),
    *((2, MATE_DOWN[half], 0, 64) for half in (0, 1)),
    (1, UP, 0, 64),
    (2, DOWN, 64, 64),
    *((2, FAR, row, 32) for row in (0, 32)),
    *((1, FAR, row, 32) for row in (64, 96)),
    *((0, MATE, row, 64) for row in (0, 64)),
    *((1, UP, row, 32) for row in (64, 96)),
    *((2, DOWN, row, 32) for row in (0, 32)),
)
PLACE = tuple(sum(message[3] for message in REDUCE[:i]) for i in range(len(REDUCE)))


class Side:
    def __init__(self, cores, near, blocks, terms, stage, landed, gather_sems, reduce_sems):
        self.cores, self.near, self.blocks = cores, near, blocks
        self.terms, self.stage, self.landed = terms, stage, landed
        self.gather_sems, self.reduce_sems = gather_sems, reduce_sems

    def rows(self, piece, row, rows):
        if isinstance(piece[0], tuple):
            piece, row = piece[row // 64], row % 64
        return pl.ds(self.cores * piece[0] + row, rows)

    def gather(self, i):
        to, source, target, row, rows = GATHER[i]
        return pltpu.make_async_remote_copy(
            src_ref=self.blocks.at[self.rows(source, row, rows)],
            dst_ref=self.blocks.at[self.rows(target, row, rows)],
            send_sem=self.gather_sems.at[0, i],
            recv_sem=self.gather_sems.at[1, i],
            device_id=self.near[to],
            device_id_type=MESH,
        )

    def send(self, *ids):
        for i in ids:
            self.gather(i).start()

    def take(self, *ids):
        for i in ids:
            self.gather(i).wait_recv()

    def place(self, i):
        return pl.ds(PLACE[i], REDUCE[i][3])

    def reduce(self, i):
        here = self.place(i)
        return pltpu.make_async_remote_copy(
            src_ref=self.stage.at[here],
            dst_ref=self.landed.at[here],
            send_sem=self.reduce_sems.at[0, i],
            recv_sem=self.reduce_sems.at[1, i],
            device_id=self.near[REDUCE[i][0]],
            device_id_type=MESH,
        )

    def arrived(self, i):
        self.reduce(i).wait_recv()
        return self.landed[self.place(i)].astype(jnp.float32)

    def give(self, i, *others):
        _, piece, row, rows = REDUCE[i]
        total = self.terms[self.rows(piece, row, rows)]
        for j in others:
            total = total + self.arrived(j)
        self.stage[self.place(i)] = total.astype(jnp.bfloat16)
        self.reduce(i).start()

    def own(self):
        top = self.terms[self.rows(OWN, 0, 64)] + self.arrived(8) + self.arrived(14)
        top = top + jnp.concatenate([self.arrived(18), self.arrived(19)], axis=0)
        bottom = self.terms[self.rows(OWN, 64, 64)] + self.arrived(9) + self.arrived(15)
        bottom = bottom + jnp.concatenate([self.arrived(16), self.arrived(17)], axis=0)
        return jnp.concatenate([top, bottom], axis=0)

    def finish(self):
        for i in range(len(GATHER)):
            self.gather(i).wait_send()
        for i in range(len(REDUCE)):
            self.reduce(i).wait_send()


def kernel(
    log_scale_ref, bias_ref, counts_ref, texts_hbm, clips_hbm,
    pool_ref, text_ref,
    texts, clips, vids, txts, coef,
    vid_unit, vid_norm, count_col, txt_unit, txt_norm,
    vid_terms, txt_terms, vid_stage, vid_landed, txt_stage, txt_landed, sib_stage, sib_landed,
    load_sems, vid_gather, vid_reduce, txt_gather, txt_reduce, sib_gather, sib_reduce,
):
    places = Places()
    barrier = pltpu.get_barrier_semaphore()
    for near in places.all():
        pl.semaphore_signal(barrier, inc=1, device_id=near, device_id_type=MESH)
    load_texts = pltpu.make_async_copy(texts_hbm, texts, load_sems.at[0])
    load_clips = pltpu.make_async_copy(clips_hbm, clips, load_sems.at[1])
    load_texts.start()
    load_clips.start()

    vid = Side(1, places.vid, vids, vid_terms, vid_stage, vid_landed, vid_gather, vid_reduce)
    txt = Side(2, places.txt, txts, txt_terms, txt_stage, txt_landed, txt_gather, txt_reduce)

    def to_sibling(piece):
        first, rows = piece
        return pltpu.make_async_remote_copy(
            src_ref=txts.at[pl.ds(2 * first, rows)],
            dst_ref=txts.at[pl.ds(2 * first + rows, rows)],
            send_sem=sib_gather.at[0, PIECES.index(piece)],
            recv_sem=sib_gather.at[1, PIECES.index(piece)],
            device_id=places.sibling,
            device_id_type=MESH,
        )

    def terms_to_sibling(piece):
        return pltpu.make_async_remote_copy(
            src_ref=sib_stage.at[pl.ds(*piece)],
            dst_ref=sib_landed.at[pl.ds(*piece)],
            send_sem=sib_reduce.at[0, PIECES.index(piece)],
            recv_sem=sib_reduce.at[1, PIECES.index(piece)],
            device_id=places.sibling,
            device_id_type=MESH,
        )

    scale = jnp.exp(jnp.full((1, 1), log_scale_ref[0], jnp.float32))
    bias = bias_ref[0]

    load_texts.wait()
    text_f = texts[...].astype(jnp.float32)
    norm = jnp.sqrt(jnp.sum(text_f * text_f, axis=1, keepdims=True) + EPS)
    unit = text_f / norm
    txt_unit[...] = unit
    txt_norm[...] = norm
    txts[pl.ds(0, ROWS)] = unit.astype(jnp.bfloat16)

    wide = jnp.broadcast_to(counts_ref[...].astype(jnp.float32), (ROWS, ROWS))
    column = jnp.transpose(wide)[:, 0:1]
    count_col[...] = column
    shape = (ROWS, ROWS * SLOTS)
    slot = lax.broadcasted_iota(jnp.int32, shape, 1)
    video = lax.broadcasted_iota(jnp.int32, shape, 0)
    slot = slot - video * SLOTS
    used = jnp.logical_and(slot >= 0, slot.astype(jnp.float32) < column)
    load_clips.wait()
    pooled = jnp.dot(
        used.astype(jnp.float32).astype(jnp.bfloat16), clips[...], preferred_element_type=jnp.float32
    ) / column
    norm = jnp.sqrt(jnp.sum(pooled * pooled, axis=1, keepdims=True) + EPS)
    unit = pooled / norm
    vid_unit[...] = unit
    vid_norm[...] = norm
    vids[pl.ds(0, ROWS)] = unit.astype(jnp.bfloat16)

    pl.semaphore_wait(barrier, len(places.all()))
    for side in (txt, vid):
        side.send(0, 3, 6)
    to_sibling(OWN).start()
    for side in (txt, vid):
        side.send(1, 4, 2, 5, 7)

    def coefs(first, stop, left, right, own=False):
        rows, columns = pl.ds(first, stop - first), pl.ds(left, right - left)
        dots = lax.dot_general(
            vids[rows], txts[columns], (((1,), (1,)), ((), ())), preferred_element_type=jnp.float32
        )
        logits = scale * dots + bias
        values = 1.0 / (1.0 + jnp.exp(-logits))
        if own:
            row = lax.broadcasted_iota(jnp.int32, (ROWS, ROWS), 0)
            col = lax.broadcasted_iota(jnp.int32, (ROWS, ROWS), 1)
            corner = values[:ROWS, :ROWS] - (row == col).astype(jnp.float32)
            coef[pl.ds(0, ROWS), pl.ds(0, ROWS)] = corner.astype(jnp.bfloat16)
            coef[pl.ds(0, ROWS), pl.ds(ROWS, right - ROWS)] = values[:ROWS, ROWS:].astype(jnp.bfloat16)
            coef[pl.ds(ROWS, stop - ROWS), columns] = values[ROWS:].astype(jnp.bfloat16)
        else:
            coef[rows, columns] = values.astype(jnp.bfloat16)

    def vid_back(first, stop, left, right, add=False):
        rows, columns = pl.ds(first, stop - first), pl.ds(left, right - left)
        terms = jnp.dot(coef[rows, columns], txts[columns], preferred_element_type=jnp.float32)
        vid_terms[rows] = vid_terms[rows] + terms if add else terms

    def txt_back(left, right, first, stop, add=False):
        rows, columns = pl.ds(first, stop - first), pl.ds(left, right - left)
        terms = lax.dot_general(
            coef[rows, columns], vids[rows], (((0,), (0,)), ((), ())), preferred_element_type=jnp.float32
        )
        txt_terms[columns] = txt_terms[columns] + terms if add else terms

    def hand_over(*pieces):
        for piece in pieces:
            first, rows = piece
            sib_stage[pl.ds(*piece)] = txt_terms[pl.ds(2 * first + rows, rows)].astype(jnp.bfloat16)
            terms_to_sibling(piece).start()

    def join(*pieces):
        for piece in pieces:
            first, rows = piece
            terms_to_sibling(piece).wait_recv()
            here = pl.ds(2 * first, rows)
            txt_terms[here] = txt_terms[here] + sib_landed[pl.ds(*piece)].astype(jnp.float32)

    sides = (txt, vid)
    early, middle, every = 2 * EARLY, 2 * MIDDLE, 2 * ALL

    for first, second in ((0, 8), (3, 10), (1, 9), (4, 11)):
        for side in sides:
            side.take(first)
            side.send(second)
    for side in sides:
        side.take(6)
        side.send(12, 14)
    for side in sides:
        side.take(7)
        side.send(13, 15)
    to_sibling(MATE).start()
    txt.take(2, 5)
    to_sibling(UP).start()
    to_sibling(DOWN).start()
    vid.take(2, 5)
    to_sibling(OWN).wait_recv()
    to_sibling(MATE).wait_recv()
    coefs(0, 512, 0, 512, own=True)
    for first, second in ((8, 16), (10, 17), (9, 18), (11, 19)):
        for side in sides:
            side.take(first)
            side.send(second)
    to_sibling(FAR).start()
    to_sibling(UP).wait_recv()
    to_sibling(DOWN).wait_recv()
    coefs(0, 512, 512, 1024)
    vid_back(0, 512, 0, 1024)
    txt.take(12, 14)
    to_sibling(MATE_UP[0]).start()
    to_sibling(MATE_DOWN[0]).start()
    vid.take(12, 14)
    txt_back(0, 1024, 0, 512)
    to_sibling(FAR).wait_recv()
    coefs(512, MIDDLE, 0, 1024)
    to_sibling(MATE_UP[0]).wait_recv()
    to_sibling(MATE_DOWN[0]).wait_recv()
    coefs(0, MIDDLE, 1024, middle)
    txt.take(13, 15, 16, 17, 18, 19)
    for piece in (MATE_UP[1], MATE_DOWN[1], MATE_FAR):
        to_sibling(piece).start()
    vid.take(13, 15, 16, 17, 18, 19)

    coefs(MIDDLE, ALL, 0, middle)
    txt_back(early, middle, 0, ALL)
    hand_over(MATE_UP[0], MATE_DOWN[0])
    for piece in (MATE_UP[1], MATE_DOWN[1], MATE_FAR):
        to_sibling(piece).wait_recv()
    coefs(EARLY, ALL, middle, every)
    vid_back(EARLY, MIDDLE, 0, every)
    vid.give(4)
    vid.give(6)
    join(MATE_UP[0], MATE_DOWN[0])
    txt.give(4)
    txt.give(6)
    coefs(0, EARLY, middle, every)
    txt_back(middle, every, 0, ALL)
    hand_over(MATE_FAR, MATE_UP[1], MATE_DOWN[1])
    vid_back(MIDDLE, ALL, 0, every)
    for i in (0, 1, 2, 3, 5, 7):
        vid.give(i)
    join(MATE_FAR, MATE_UP[1], MATE_DOWN[1])
    for i in (0, 1, 2, 3, 5, 7):
        txt.give(i)
    vid_back(0, 512, 1024, every, add=True)
    vid.give(8)
    vid.give(9)
    txt_back(0, 1024, 512, ALL, add=True)
    hand_over(UP, DOWN, MATE, OWN)
    vid_back(512, EARLY, 0, every)
    for i, other in ((10, 0), (12, 1), (11, 2), (13, 3)):
        vid.give(i, other)
    txt_back(1024, early, 0, ALL)
    hand_over(FAR)
    join(UP, DOWN)
    txt.give(8)
    txt.give(9)
    join(FAR)
    for i, other in ((10, 0), (12, 1), (11, 2), (13, 3)):
        txt.give(i, other)
    vid.give(14, 4, 6)
    vid.give(15, 5, 7)
    join(MATE)
    txt.give(14, 4, 6)
    txt.give(15, 5, 7)
    for i, other in ((18, 10), (16, 12), (19, 11), (17, 13)):
        vid.give(i, other)
    for i, other in ((18, 10), (16, 12), (19, 11), (17, 13)):
        txt.give(i, other)

    back = scale * vid.own()
    unit = vid_unit[...]
    back = (back - unit * jnp.sum(unit * back, axis=1, keepdims=True)) / vid_norm[...]
    pool_ref[...] = back / count_col[...]
    join(OWN)
    back = scale * txt.own()
    unit = txt_unit[...]
    text_ref[...] = (back - unit * jnp.sum(unit * back, axis=1, keepdims=True)) / txt_norm[...]

    vid.finish()
    txt.finish()
    for piece in PIECES:
        to_sibling(piece).wait_send()
        terms_to_sibling(piece).wait_send()


def spread(counts_ref, pool_hbm, text_hbm, clip_hbm, text_out, pool, text, clip, load_sems, store_sems):
    videos, slots, width = clip.shape
    parts = store_sems.shape[0] - 1
    step = videos // parts
    load_text = pltpu.make_async_copy(text_hbm, text, load_sems.at[parts])
    store_text = pltpu.make_async_copy(text, text_out, store_sems.at[parts])

    def part(i):
        return pl.ds(i * step, step)

    def load(i):
        return pltpu.make_async_copy(pool_hbm.at[part(i)], pool.at[part(i)], load_sems.at[i])

    def store(i):
        return pltpu.make_async_copy(clip.at[part(i)], clip_hbm.at[part(i)], store_sems.at[i])

    for i in range(parts):
        load(i).start()
    load_text.start()
    slot = lax.broadcasted_iota(jnp.int32, (slots, width), 0)
    for i in range(parts):
        load(i).wait()
        for video in range(i * step, (i + 1) * step):
            row = jnp.broadcast_to(pool[pl.ds(video, 1)], (slots, width))
            clip[video] = jnp.where(slot < counts_ref[video], row, 0.0)
        store(i).start()
    load_text.wait()
    store_text.start()
    for i in range(parts):
        store(i).wait()
    store_text.wait()


def on_device(clips, counts, texts, log_scale, bias):
    videos, slots, width = clips.shape
    bf16, f32 = jnp.bfloat16, jnp.float32
    smem = pl.BlockSpec(memory_space=pltpu.SMEM)
    vmem = pl.BlockSpec(memory_space=pltpu.VMEM)
    hbm = pl.BlockSpec(memory_space=pl.ANY)
    dma = pltpu.SemaphoreType.DMA
    own = jax.ShapeDtypeStruct((videos, width), f32)
    pool_grad, text_grad = pl.pallas_call(
        kernel,
        out_shape=(own, own),
        in_specs=[smem, smem, vmem, hbm, hbm],
        out_specs=(vmem, vmem),
        scratch_shapes=[
            pltpu.VMEM((ROWS, width), bf16),
            pltpu.VMEM((ROWS * SLOTS, width), bf16),
            pltpu.VMEM((BLOCKS * ROWS, width), bf16),
            pltpu.VMEM((2 * BLOCKS * ROWS, width), bf16),
            pltpu.VMEM((BLOCKS * ROWS, 2 * BLOCKS * ROWS), bf16),
            pltpu.VMEM((ROWS, width), f32),
            pltpu.VMEM((ROWS, 1), f32),
            pltpu.VMEM((ROWS, 1), f32),
            pltpu.VMEM((ROWS, width), f32),
            pltpu.VMEM((ROWS, 1), f32),
            pltpu.VMEM((BLOCKS * ROWS, width), f32),
            pltpu.VMEM((2 * BLOCKS * ROWS, width), f32),
            pltpu.VMEM(((BLOCKS - 1) * ROWS, width), bf16),
            pltpu.VMEM(((BLOCKS - 1) * ROWS, width), bf16),
            pltpu.VMEM(((BLOCKS - 1) * ROWS, width), bf16),
            pltpu.VMEM(((BLOCKS - 1) * ROWS, width), bf16),
            pltpu.VMEM((BLOCKS * ROWS, width), bf16),
            pltpu.VMEM((BLOCKS * ROWS, width), bf16),
            dma((2,)),
            dma((2, len(GATHER))),
            dma((2, len(REDUCE))),
            dma((2, len(GATHER))),
            dma((2, len(REDUCE))),
            dma((2, len(PIECES))),
            dma((2, len(PIECES))),
        ],
        compiler_params=pltpu.CompilerParams(
            collective_id=0, has_side_effects=True, vmem_limit_bytes=60 * 1024 * 1024
        ),
        cost_estimate=pl.CostEstimate(
            flops=6 * 1024 * 2048 * width, bytes_accessed=4 * 1024 * 1024, transcendentals=2 * 1024 * 2048
        ),
    )(log_scale, bias, counts.reshape(1, videos), texts, clips.reshape(videos * slots, width))
    return pl.pallas_call(
        spread,
        out_shape=(jax.ShapeDtypeStruct((videos, slots, width), f32), own),
        in_specs=[smem, hbm, hbm],
        out_specs=(hbm, hbm),
        scratch_shapes=[
            pltpu.VMEM((videos, width), f32),
            pltpu.VMEM((videos, width), f32),
            pltpu.VMEM((videos, slots, width), f32),
            dma((5,)),
            dma((5,)),
        ],
        compiler_params=pltpu.CompilerParams(vmem_limit_bytes=60 * 1024 * 1024),
        cost_estimate=pl.CostEstimate(flops=0, bytes_accessed=6 * 1024 * 1024, transcendentals=0),
    )(counts, pool_grad, text_grad)


def solution(mesh):
    return jax.shard_map(
        on_device,
        mesh=mesh,
        in_specs=(
            P(("group", "inner"), None, None),
            P(("group", "inner")),
            P(("group", "inner"), None),
            P(),
            P(),
        ),
        out_specs=(P(("group", "inner"), None, None), P(("group", "inner"), None)),
        check_vma=False,
    )
```

```python
import functools

import jax
import jax.numpy as jnp
from jax import lax
from jax.experimental import pallas as pl
from jax.experimental.pallas import tpu as pltpu
from jax.sharding import PartitionSpec as P

MESH = pl.DeviceIdType.MESH
ROWS = 128
SLOTS = 8
BLOCKS = 8
EPS = 1e-06

OWN, MATE, UP, DOWN, FAR = ((i * ROWS, ROWS) for i in range(5))
MATE_UP = ((640, 64), (768, 64))
MATE_DOWN = ((704, 64), (832, 64))
MATE_FAR = (896, ROWS)
PIECES = (OWN, MATE, UP, DOWN, FAR, MATE_UP[0], MATE_DOWN[0], MATE_UP[1], MATE_DOWN[1], MATE_FAR)
EARLY, MIDDLE, FIRST, ALL = 640, 768, 896, 1024


def device_at(x, y, z, core):
    return ((x % 2) * 8 + z * 2 + core, y * 2 + x // 2)


class Places:
    def __init__(self):
        group, inner = lax.axis_index("group"), lax.axis_index("inner")
        core, z, y = group % 2, (group // 2) % 4, inner // 2
        x = (inner % 2) * 2 + group // 8
        odd = x % 2
        self.sibling = device_at(x, y, z, 1 - core)
        self.vid = (
            device_at(x + 1 - 2 * odd, y, z, core),
            device_at(x, (y + 1) % 4, z, core),
            device_at(x, (y + 3) % 4, z, core),
        )
        self.txt = (
            device_at((x + 3 + 2 * odd) % 4, y, z, core),
            device_at(x, y, (z + 1) % 4, core),
            device_at(x, y, (z + 3) % 4, core),
        )

    def all(self):
        return (self.sibling, *self.vid, *self.txt)


GATHER = (
    *((1, OWN, DOWN, row, rows) for row, rows in ((0, 32), (32, 32), (64, 64))),
    *((2, OWN, UP, row, rows) for row, rows in ((64, 32), (96, 32), (0, 64))),
    *((0, OWN, MATE, row, 64) for row in (0, 64)),
    *((1, DOWN, FAR, row, 32) for row in (0, 32)),
    *((2, UP, FAR, row, 32) for row in (64, 96)),
    *((1, MATE, MATE_DOWN, row, 64) for row in (0, 64)),
    *((2, MATE, MATE_UP, row, 64) for row in (0, 64)),
    *((0, FAR, MATE_FAR, row, 32) for row in (0, 64, 32, 96)),
)
REDUCE = (
    *((0, MATE_FAR, row, 32) for row in (0, 64, 32, 96)),
    *((1, MATE_UP[half], 0, 64) for half in (0, 1)),
    *((2, MATE_DOWN[half], 0, 64) for half in (0, 1)),
    (1, UP, 0, 64),
    (2, DOWN, 64, 64),
    *((2, FAR, row, 32) for row in (0, 32)),
    *((1, FAR, row, 32) for row in (64, 96)),
    *((0, MATE, row, 64) for row in (0, 64)),
    *((1, UP, row, 32) for row in (64, 96)),
    *((2, DOWN, row, 32) for row in (0, 32)),
)
PLACE = tuple(sum(message[3] for message in REDUCE[:i]) for i in range(len(REDUCE)))


class Side:
    def __init__(self, cores, near, blocks, terms, stage, landed, gather_sems, reduce_sems):
        self.cores, self.near, self.blocks = cores, near, blocks
        self.terms, self.stage, self.landed = terms, stage, landed
        self.gather_sems, self.reduce_sems = gather_sems, reduce_sems

    def rows(self, piece, row, rows):
        if isinstance(piece[0], tuple):
            piece, row = piece[row // 64], row % 64
        return pl.ds(self.cores * piece[0] + row, rows)

    def gather(self, i):
        to, source, target, row, rows = GATHER[i]
        return pltpu.make_async_remote_copy(
            src_ref=self.blocks.at[self.rows(source, row, rows)],
            dst_ref=self.blocks.at[self.rows(target, row, rows)],
            send_sem=self.gather_sems.at[0, i],
            recv_sem=self.gather_sems.at[1, i],
            device_id=self.near[to],
            device_id_type=MESH,
        )

    def send(self, *ids):
        for i in ids:
            self.gather(i).start()

    def take(self, *ids):
        for i in ids:
            self.gather(i).wait_recv()

    def place(self, i):
        return pl.ds(PLACE[i], REDUCE[i][3])

    def reduce(self, i):
        here = self.place(i)
        return pltpu.make_async_remote_copy(
            src_ref=self.stage.at[here],
            dst_ref=self.landed.at[here],
            send_sem=self.reduce_sems.at[0, i],
            recv_sem=self.reduce_sems.at[1, i],
            device_id=self.near[REDUCE[i][0]],
            device_id_type=MESH,
        )

    def arrived(self, i):
        self.reduce(i).wait_recv()
        return self.landed[self.place(i)].astype(jnp.float32)

    def give(self, i, *others):
        _, piece, row, rows = REDUCE[i]
        total = self.terms[self.rows(piece, row, rows)]
        for j in others:
            total = total + self.arrived(j)
        self.stage[self.place(i)] = total.astype(jnp.bfloat16)
        self.reduce(i).start()

    def own(self):
        top = self.terms[self.rows(OWN, 0, 64)] + self.arrived(8) + self.arrived(14)
        top = top + jnp.concatenate([self.arrived(18), self.arrived(19)], axis=0)
        bottom = self.terms[self.rows(OWN, 64, 64)] + self.arrived(9) + self.arrived(15)
        bottom = bottom + jnp.concatenate([self.arrived(16), self.arrived(17)], axis=0)
        return jnp.concatenate([top, bottom], axis=0)

    def finish(self):
        for i in range(len(GATHER)):
            self.gather(i).wait_send()
        for i in range(len(REDUCE)):
            self.reduce(i).wait_send()


def kernel(
    log_scale_ref, bias_ref, counts_ref, texts_hbm, clips_hbm,
    pool_ref, text_ref,
    texts, clips, vids, txts, coef,
    vid_unit, vid_norm, count_col, txt_unit, txt_norm,
    vid_terms, txt_terms, vid_stage, vid_landed, txt_stage, txt_landed, sib_stage, sib_landed,
    load_sems, vid_gather, vid_reduce, txt_gather, txt_reduce, sib_gather, sib_reduce,
):
    places = Places()
    barrier = pltpu.get_barrier_semaphore()
    for near in places.all():
        pl.semaphore_signal(barrier, inc=1, device_id=near, device_id_type=MESH)
    load_texts = pltpu.make_async_copy(texts_hbm, texts, load_sems.at[0])
    load_clips = pltpu.make_async_copy(clips_hbm, clips, load_sems.at[1])
    load_texts.start()
    load_clips.start()

    vid = Side(1, places.vid, vids, vid_terms, vid_stage, vid_landed, vid_gather, vid_reduce)
    txt = Side(2, places.txt, txts, txt_terms, txt_stage, txt_landed, txt_gather, txt_reduce)

    def to_sibling(piece):
        first, rows = piece
        return pltpu.make_async_remote_copy(
            src_ref=txts.at[pl.ds(2 * first, rows)],
            dst_ref=txts.at[pl.ds(2 * first + rows, rows)],
            send_sem=sib_gather.at[0, PIECES.index(piece)],
            recv_sem=sib_gather.at[1, PIECES.index(piece)],
            device_id=places.sibling,
            device_id_type=MESH,
        )

    def terms_to_sibling(piece):
        return pltpu.make_async_remote_copy(
            src_ref=sib_stage.at[pl.ds(*piece)],
            dst_ref=sib_landed.at[pl.ds(*piece)],
            send_sem=sib_reduce.at[0, PIECES.index(piece)],
            recv_sem=sib_reduce.at[1, PIECES.index(piece)],
            device_id=places.sibling,
            device_id_type=MESH,
        )

    scale = jnp.exp(jnp.full((1, 1), log_scale_ref[0], jnp.float32))
    bias = bias_ref[0]

    load_texts.wait()
    text_f = texts[...].astype(jnp.float32)
    norm = jnp.sqrt(jnp.sum(text_f * text_f, axis=1, keepdims=True) + EPS)
    unit = text_f / norm
    txt_unit[...] = unit
    txt_norm[...] = norm
    txts[pl.ds(0, ROWS)] = unit.astype(jnp.bfloat16)

    wide = jnp.broadcast_to(counts_ref[...].astype(jnp.float32), (ROWS, ROWS))
    column = jnp.transpose(wide)[:, 0:1]
    count_col[...] = column
    shape = (ROWS, ROWS * SLOTS)
    slot = lax.broadcasted_iota(jnp.int32, shape, 1)
    video = lax.broadcasted_iota(jnp.int32, shape, 0)
    slot = slot - video * SLOTS
    used = jnp.logical_and(slot >= 0, slot.astype(jnp.float32) < column)
    load_clips.wait()
    pooled = jnp.dot(
        used.astype(jnp.float32).astype(jnp.bfloat16), clips[...], preferred_element_type=jnp.float32
    ) / column
    norm = jnp.sqrt(jnp.sum(pooled * pooled, axis=1, keepdims=True) + EPS)
    unit = pooled / norm
    vid_unit[...] = unit
    vid_norm[...] = norm
    vids[pl.ds(0, ROWS)] = unit.astype(jnp.bfloat16)

    pl.semaphore_wait(barrier, len(places.all()))
    for side in (txt, vid):
        side.send(0, 3, 6)
    to_sibling(OWN).start()
    for side in (txt, vid):
        side.send(1, 4, 2, 5, 7)

    def coefs(first, stop, left, right, own=False):
        rows, columns = pl.ds(first, stop - first), pl.ds(left, right - left)
        dots = lax.dot_general(
            vids[rows], txts[columns], (((1,), (1,)), ((), ())), preferred_element_type=jnp.float32
        )
        logits = scale * dots + bias
        values = 1.0 / (1.0 + jnp.exp(-logits))
        if own:
            row = lax.broadcasted_iota(jnp.int32, (ROWS, ROWS), 0)
            col = lax.broadcasted_iota(jnp.int32, (ROWS, ROWS), 1)
            corner = values[:ROWS, :ROWS] - (row == col).astype(jnp.float32)
            coef[pl.ds(0, ROWS), pl.ds(0, ROWS)] = corner.astype(jnp.bfloat16)
            coef[pl.ds(0, ROWS), pl.ds(ROWS, right - ROWS)] = values[:ROWS, ROWS:].astype(jnp.bfloat16)
            coef[pl.ds(ROWS, stop - ROWS), columns] = values[ROWS:].astype(jnp.bfloat16)
        else:
            coef[rows, columns] = values.astype(jnp.bfloat16)

    def vid_back(first, stop, left, right, add=False):
        rows, columns = pl.ds(first, stop - first), pl.ds(left, right - left)
        terms = jnp.dot(coef[rows, columns], txts[columns], preferred_element_type=jnp.float32)
        vid_terms[rows] = vid_terms[rows] + terms if add else terms

    def txt_back(left, right, first, stop, add=False):
        rows, columns = pl.ds(first, stop - first), pl.ds(left, right - left)
        terms = lax.dot_general(
            coef[rows, columns], vids[rows], (((0,), (0,)), ((), ())), preferred_element_type=jnp.float32
        )
        txt_terms[columns] = txt_terms[columns] + terms if add else terms

    def hand_over(*pieces):
        for piece in pieces:
            first, rows = piece
            sib_stage[pl.ds(*piece)] = txt_terms[pl.ds(2 * first + rows, rows)].astype(jnp.bfloat16)
            terms_to_sibling(piece).start()

    def join(*pieces):
        for piece in pieces:
            first, rows = piece
            terms_to_sibling(piece).wait_recv()
            here = pl.ds(2 * first, rows)
            txt_terms[here] = txt_terms[here] + sib_landed[pl.ds(*piece)].astype(jnp.float32)

    sides = (txt, vid)
    early, middle, every = 2 * EARLY, 2 * MIDDLE, 2 * ALL

    for first, second in ((0, 8), (3, 10), (1, 9), (4, 11)):
        for side in sides:
            side.take(first)
            side.send(second)
    for side in sides:
        side.take(6)
        side.send(12, 14)
    for side in sides:
        side.take(7)
        side.send(13, 15)
    to_sibling(MATE).start()
    txt.take(2, 5)
    to_sibling(UP).start()
    to_sibling(DOWN).start()
    vid.take(2, 5)
    to_sibling(OWN).wait_recv()
    to_sibling(MATE).wait_recv()
    for first, second in ((8, 16), (10, 17)):
        for side in sides:
            side.take(first)
            side.send(second)
    coefs(0, 512, 0, 512, own=True)
    for first, second in ((9, 18), (11, 19)):
        for side in sides:
            side.take(first)
            side.send(second)
    to_sibling(FAR).start()
    to_sibling(UP).wait_recv()
    to_sibling(DOWN).wait_recv()
    coefs(0, 512, 512, 1024)
    vid_back(0, 512, 0, 1024)
    txt.take(12, 14)
    to_sibling(MATE_UP[0]).start()
    to_sibling(MATE_DOWN[0]).start()
    vid.take(12, 14)
    txt_back(0, 1024, 0, 512)
    to_sibling(FAR).wait_recv()
    coefs(512, MIDDLE, 0, 1024)
    to_sibling(MATE_UP[0]).wait_recv()
    to_sibling(MATE_DOWN[0]).wait_recv()
    coefs(0, MIDDLE, 1024, middle)
    txt.take(13, 15, 16, 17, 18, 19)
    for piece in (MATE_UP[1], MATE_DOWN[1], MATE_FAR):
        to_sibling(piece).start()
    vid.take(13, 15, 16, 17, 18, 19)

    coefs(MIDDLE, ALL, 0, middle)
    txt_back(early, middle, 0, ALL)
    hand_over(MATE_UP[0], MATE_DOWN[0])
    for piece in (MATE_UP[1], MATE_DOWN[1], MATE_FAR):
        to_sibling(piece).wait_recv()
    coefs(EARLY, ALL, middle, every)
    vid_back(EARLY, MIDDLE, 0, every)
    vid.give(4)
    vid.give(6)
    join(MATE_UP[0], MATE_DOWN[0])
    txt.give(4)
    txt.give(6)
    vid_back(FIRST, ALL, 0, every)
    for i in (0, 1, 2, 3):
        vid.give(i)
    coefs(0, EARLY, middle, every)
    txt_back(2 * FIRST, every, 0, ALL)
    hand_over(MATE_FAR)
    txt_back(middle, 2 * FIRST, 0, ALL)
    hand_over(MATE_UP[1], MATE_DOWN[1])
    join(MATE_FAR)
    for i in (0, 1, 2, 3):
        txt.give(i)
    vid_back(MIDDLE, FIRST, 0, every)
    vid.give(5)
    vid.give(7)
    join(MATE_UP[1], MATE_DOWN[1])
    txt.give(5)
    txt.give(7)
    txt_back(512, 1024, 512, ALL, add=True)
    txt_back(1024, early, 0, ALL)
    hand_over(UP, DOWN, FAR)
    vid_back(512, EARLY, 0, every)
    vid_back(0, 512, 1024, every, add=True)
    join(UP, DOWN, FAR)
    for i, other in ((10, 0), (12, 1), (11, 2), (13, 3)):
        vid.give(i, other)
    vid.give(8)
    vid.give(9)
    txt.give(10, 0)
    txt.give(12, 1)
    txt.give(8)
    txt.give(9)
    txt_back(0, 512, 512, ALL, add=True)
    hand_over(MATE, OWN)
    vid.give(14, 4, 6)
    vid.give(15, 5, 7)
    txt.give(11, 2)
    txt.give(13, 3)
    join(MATE)
    txt.give(14, 4, 6)
    txt.give(15, 5, 7)
    for i, other in ((18, 10), (16, 12), (19, 11), (17, 13)):
        for side in (vid, txt):
            side.give(i, other)

    back = scale * vid.own()
    unit = vid_unit[...]
    back = (back - unit * jnp.sum(unit * back, axis=1, keepdims=True)) / vid_norm[...]
    pool_ref[...] = back / count_col[...]
    join(OWN)
    back = scale * txt.own()
    unit = txt_unit[...]
    text_ref[...] = (back - unit * jnp.sum(unit * back, axis=1, keepdims=True)) / txt_norm[...]

    vid.finish()
    txt.finish()
    for piece in PIECES:
        to_sibling(piece).wait_send()
        terms_to_sibling(piece).wait_send()


def spread(counts_ref, pool_hbm, text_hbm, clip_hbm, text_out, pool, text, clip, load_sems, store_sems):
    videos, slots, width = clip.shape
    parts = store_sems.shape[0] - 1
    step = videos // parts
    load_text = pltpu.make_async_copy(text_hbm, text, load_sems.at[parts])
    store_text = pltpu.make_async_copy(text, text_out, store_sems.at[parts])

    def part(i):
        return pl.ds(i * step, step)

    def load(i):
        return pltpu.make_async_copy(pool_hbm.at[part(i)], pool.at[part(i)], load_sems.at[i])

    def store(i):
        return pltpu.make_async_copy(clip.at[part(i)], clip_hbm.at[part(i)], store_sems.at[i])

    for i in range(parts):
        load(i).start()
    load_text.start()
    slot = lax.broadcasted_iota(jnp.int32, (slots, width), 0)
    for i in range(parts):
        load(i).wait()
        for video in range(i * step, (i + 1) * step):
            row = jnp.broadcast_to(pool[pl.ds(video, 1)], (slots, width))
            clip[video] = jnp.where(slot < counts_ref[video], row, 0.0)
        store(i).start()
    load_text.wait()
    store_text.start()
    for i in range(parts):
        store(i).wait()
    store_text.wait()


def on_device(clips, counts, texts, log_scale, bias):
    videos, slots, width = clips.shape
    bf16, f32 = jnp.bfloat16, jnp.float32
    smem = pl.BlockSpec(memory_space=pltpu.SMEM)
    vmem = pl.BlockSpec(memory_space=pltpu.VMEM)
    hbm = pl.BlockSpec(memory_space=pl.ANY)
    dma = pltpu.SemaphoreType.DMA
    own = jax.ShapeDtypeStruct((videos, width), f32)
    pool_grad, text_grad = pl.pallas_call(
        kernel,
        out_shape=(own, own),
        in_specs=[smem, smem, vmem, hbm, hbm],
        out_specs=(vmem, vmem),
        scratch_shapes=[
            pltpu.VMEM((ROWS, width), bf16),
            pltpu.VMEM((ROWS * SLOTS, width), bf16),
            pltpu.VMEM((BLOCKS * ROWS, width), bf16),
            pltpu.VMEM((2 * BLOCKS * ROWS, width), bf16),
            pltpu.VMEM((BLOCKS * ROWS, 2 * BLOCKS * ROWS), bf16),
            pltpu.VMEM((ROWS, width), f32),
            pltpu.VMEM((ROWS, 1), f32),
            pltpu.VMEM((ROWS, 1), f32),
            pltpu.VMEM((ROWS, width), f32),
            pltpu.VMEM((ROWS, 1), f32),
            pltpu.VMEM((BLOCKS * ROWS, width), f32),
            pltpu.VMEM((2 * BLOCKS * ROWS, width), f32),
            pltpu.VMEM(((BLOCKS - 1) * ROWS, width), bf16),
            pltpu.VMEM(((BLOCKS - 1) * ROWS, width), bf16),
            pltpu.VMEM(((BLOCKS - 1) * ROWS, width), bf16),
            pltpu.VMEM(((BLOCKS - 1) * ROWS, width), bf16),
            pltpu.VMEM((BLOCKS * ROWS, width), bf16),
            pltpu.VMEM((BLOCKS * ROWS, width), bf16),
            dma((2,)),
            dma((2, len(GATHER))),
            dma((2, len(REDUCE))),
            dma((2, len(GATHER))),
            dma((2, len(REDUCE))),
            dma((2, len(PIECES))),
            dma((2, len(PIECES))),
        ],
        compiler_params=pltpu.CompilerParams(
            collective_id=0, has_side_effects=True, vmem_limit_bytes=60 * 1024 * 1024
        ),
        cost_estimate=pl.CostEstimate(
            flops=6 * 1024 * 2048 * width, bytes_accessed=4 * 1024 * 1024, transcendentals=2 * 1024 * 2048
        ),
    )(log_scale, bias, counts.reshape(1, videos), texts, clips.reshape(videos * slots, width))
    return pl.pallas_call(
        spread,
        out_shape=(jax.ShapeDtypeStruct((videos, slots, width), f32), own),
        in_specs=[smem, hbm, hbm],
        out_specs=(hbm, hbm),
        scratch_shapes=[
            pltpu.VMEM((videos, width), f32),
            pltpu.VMEM((videos, width), f32),
            pltpu.VMEM((videos, slots, width), f32),
            dma((5,)),
            dma((5,)),
        ],
        compiler_params=pltpu.CompilerParams(vmem_limit_bytes=60 * 1024 * 1024),
        cost_estimate=pl.CostEstimate(flops=0, bytes_accessed=6 * 1024 * 1024, transcendentals=0),
    )(counts, pool_grad, text_grad)


def solution(mesh):
    return jax.shard_map(
        on_device,
        mesh=mesh,
        in_specs=(
            P(("group", "inner"), None, None),
            P(("group", "inner")),
            P(("group", "inner"), None),
            P(),
            P(),
        ),
        out_specs=(P(("group", "inner"), None, None), P(("group", "inner"), None)),
        check_vma=False,
    )
```

```python
import functools

import jax
import jax.numpy as jnp
from jax import lax
from jax.experimental import pallas as pl
from jax.experimental.pallas import tpu as pltpu
from jax.sharding import PartitionSpec as P

MESH = pl.DeviceIdType.MESH
ROWS = 128
SLOTS = 8
BLOCKS = 8
EPS = 1e-06

OWN, MATE, UP, DOWN, FAR = ((i * ROWS, ROWS) for i in range(5))
MATE_UP = ((640, 64), (768, 64))
MATE_DOWN = ((704, 64), (832, 64))
MATE_FAR = (896, ROWS)
PIECES = (OWN, MATE, UP, DOWN, FAR, MATE_UP[0], MATE_DOWN[0], MATE_UP[1], MATE_DOWN[1], MATE_FAR)
EARLY, MIDDLE, FIRST, ALL = 640, 768, 896, 1024


def device_at(x, y, z, core):
    return ((x % 2) * 8 + z * 2 + core, y * 2 + x // 2)


class Places:
    def __init__(self):
        group, inner = lax.axis_index("group"), lax.axis_index("inner")
        core, z, y = group % 2, (group // 2) % 4, inner // 2
        x = (inner % 2) * 2 + group // 8
        odd = x % 2
        self.sibling = device_at(x, y, z, 1 - core)
        self.vid = (
            device_at(x + 1 - 2 * odd, y, z, core),
            device_at(x, (y + 1) % 4, z, core),
            device_at(x, (y + 3) % 4, z, core),
        )
        self.txt = (
            device_at((x + 3 + 2 * odd) % 4, y, z, core),
            device_at(x, y, (z + 1) % 4, core),
            device_at(x, y, (z + 3) % 4, core),
        )

    def all(self):
        return (self.sibling, *self.vid, *self.txt)


GATHER = (
    *((1, OWN, DOWN, row, rows) for row, rows in ((0, 32), (32, 32), (64, 64))),
    *((2, OWN, UP, row, rows) for row, rows in ((64, 32), (96, 32), (0, 64))),
    *((0, OWN, MATE, row, 64) for row in (0, 64)),
    *((1, DOWN, FAR, row, 32) for row in (0, 32)),
    *((2, UP, FAR, row, 32) for row in (64, 96)),
    *((1, MATE, MATE_DOWN, row, 64) for row in (0, 64)),
    *((2, MATE, MATE_UP, row, 64) for row in (0, 64)),
    *((0, FAR, MATE_FAR, row, 32) for row in (0, 64, 32, 96)),
)
REDUCE = (
    *((0, MATE_FAR, row, 32) for row in (0, 64, 32, 96)),
    *((1, MATE_UP[half], 0, 64) for half in (0, 1)),
    *((2, MATE_DOWN[half], 0, 64) for half in (0, 1)),
    (1, UP, 0, 64),
    (2, DOWN, 64, 64),
    *((2, FAR, row, 32) for row in (0, 32)),
    *((1, FAR, row, 32) for row in (64, 96)),
    *((0, MATE, row, 64) for row in (0, 64)),
    *((1, UP, row, 32) for row in (64, 96)),
    *((2, DOWN, row, 32) for row in (0, 32)),
)
PLACE = tuple(sum(message[3] for message in REDUCE[:i]) for i in range(len(REDUCE)))


class Side:
    def __init__(self, cores, near, blocks, terms, stage, landed, gather_sems, reduce_sems):
        self.cores, self.near, self.blocks = cores, near, blocks
        self.terms, self.stage, self.landed = terms, stage, landed
        self.gather_sems, self.reduce_sems = gather_sems, reduce_sems

    def rows(self, piece, row, rows):
        if isinstance(piece[0], tuple):
            piece, row = piece[row // 64], row % 64
        return pl.ds(self.cores * piece[0] + row, rows)

    def gather(self, i):
        to, source, target, row, rows = GATHER[i]
        return pltpu.make_async_remote_copy(
            src_ref=self.blocks.at[self.rows(source, row, rows)],
            dst_ref=self.blocks.at[self.rows(target, row, rows)],
            send_sem=self.gather_sems.at[0, i],
            recv_sem=self.gather_sems.at[1, i],
            device_id=self.near[to],
            device_id_type=MESH,
        )

    def send(self, *ids):
        for i in ids:
            self.gather(i).start()

    def take(self, *ids):
        for i in ids:
            self.gather(i).wait_recv()

    def place(self, i):
        return pl.ds(PLACE[i], REDUCE[i][3])

    def reduce(self, i):
        here = self.place(i)
        return pltpu.make_async_remote_copy(
            src_ref=self.stage.at[here],
            dst_ref=self.landed.at[here],
            send_sem=self.reduce_sems.at[0, i],
            recv_sem=self.reduce_sems.at[1, i],
            device_id=self.near[REDUCE[i][0]],
            device_id_type=MESH,
        )

    def arrived(self, i):
        self.reduce(i).wait_recv()
        return self.landed[self.place(i)].astype(jnp.float32)

    def give(self, i, *others):
        _, piece, row, rows = REDUCE[i]
        total = self.terms[self.rows(piece, row, rows)]
        for j in others:
            total = total + self.arrived(j)
        self.stage[self.place(i)] = total.astype(jnp.bfloat16)
        self.reduce(i).start()

    def own(self):
        top = self.terms[self.rows(OWN, 0, 64)] + self.arrived(8) + self.arrived(14)
        top = top + jnp.concatenate([self.arrived(18), self.arrived(19)], axis=0)
        bottom = self.terms[self.rows(OWN, 64, 64)] + self.arrived(9) + self.arrived(15)
        bottom = bottom + jnp.concatenate([self.arrived(16), self.arrived(17)], axis=0)
        return jnp.concatenate([top, bottom], axis=0)

    def finish(self):
        for i in range(len(GATHER)):
            self.gather(i).wait_send()
        for i in range(len(REDUCE)):
            self.reduce(i).wait_send()


def kernel(
    log_scale_ref, bias_ref, counts_ref, texts_hbm, clips_hbm,
    pool_ref, text_ref,
    texts, clips, vids, txts, coef, pool,
    vid_unit, vid_norm, count_col, txt_unit, txt_norm,
    vid_terms, txt_terms, vid_stage, vid_landed, txt_stage, txt_landed, sib_stage, sib_landed,
    load_sems, vid_gather, vid_reduce, txt_gather, txt_reduce, sib_gather, sib_reduce,
):
    places = Places()
    barrier = pltpu.get_barrier_semaphore()
    for near in places.all():
        pl.semaphore_signal(barrier, inc=1, device_id=near, device_id_type=MESH)
    load_texts = pltpu.make_async_copy(texts_hbm, texts, load_sems.at[0])
    load_clips = pltpu.make_async_copy(clips_hbm, clips, load_sems.at[1])
    load_texts.start()
    load_clips.start()

    vid = Side(1, places.vid, vids, vid_terms, vid_stage, vid_landed, vid_gather, vid_reduce)
    txt = Side(2, places.txt, txts, txt_terms, txt_stage, txt_landed, txt_gather, txt_reduce)

    def to_sibling(piece):
        first, rows = piece
        return pltpu.make_async_remote_copy(
            src_ref=txts.at[pl.ds(2 * first, rows)],
            dst_ref=txts.at[pl.ds(2 * first + rows, rows)],
            send_sem=sib_gather.at[0, PIECES.index(piece)],
            recv_sem=sib_gather.at[1, PIECES.index(piece)],
            device_id=places.sibling,
            device_id_type=MESH,
        )

    def terms_to_sibling(piece):
        return pltpu.make_async_remote_copy(
            src_ref=sib_stage.at[pl.ds(*piece)],
            dst_ref=sib_landed.at[pl.ds(*piece)],
            send_sem=sib_reduce.at[0, PIECES.index(piece)],
            recv_sem=sib_reduce.at[1, PIECES.index(piece)],
            device_id=places.sibling,
            device_id_type=MESH,
        )

    scale = jnp.exp(jnp.full((1, 1), log_scale_ref[0], jnp.float32))
    bias = bias_ref[0]

    load_texts.wait()
    text_f = texts[...].astype(jnp.float32)
    norm = jnp.sqrt(jnp.sum(text_f * text_f, axis=1, keepdims=True) + EPS)
    unit = text_f / norm
    txt_unit[...] = unit
    txt_norm[...] = norm
    txts[pl.ds(0, ROWS)] = unit.astype(jnp.bfloat16)

    wide = jnp.broadcast_to(counts_ref[...].astype(jnp.float32), (ROWS, ROWS))
    column = jnp.transpose(wide)[:, 0:1]
    count_col[...] = column
    shape = (ROWS, ROWS * SLOTS)
    slot = lax.broadcasted_iota(jnp.int32, shape, 1)
    video = lax.broadcasted_iota(jnp.int32, shape, 0)
    slot = slot - video * SLOTS
    used = jnp.logical_and(slot >= 0, slot.astype(jnp.float32) < column)
    load_clips.wait()
    pooled = jnp.dot(
        used.astype(jnp.float32).astype(jnp.bfloat16), clips[...], preferred_element_type=jnp.float32
    ) / column
    norm = jnp.sqrt(jnp.sum(pooled * pooled, axis=1, keepdims=True) + EPS)
    unit = pooled / norm
    vid_unit[...] = unit
    vid_norm[...] = norm
    vids[pl.ds(0, ROWS)] = unit.astype(jnp.bfloat16)

    pl.semaphore_wait(barrier, len(places.all()))
    for side in (txt, vid):
        side.send(0, 3, 6)
    to_sibling(OWN).start()
    for side in (txt, vid):
        side.send(1, 4, 2, 5, 7)

    def coefs(first, stop, left, right, own=False):
        rows, columns = pl.ds(first, stop - first), pl.ds(left, right - left)
        dots = lax.dot_general(
            vids[rows], txts[columns], (((1,), (1,)), ((), ())), preferred_element_type=jnp.float32
        )
        logits = scale * dots + bias
        values = 1.0 / (1.0 + jnp.exp(-logits))
        if own:
            row = lax.broadcasted_iota(jnp.int32, (ROWS, ROWS), 0)
            col = lax.broadcasted_iota(jnp.int32, (ROWS, ROWS), 1)
            corner = values[:ROWS, :ROWS] - (row == col).astype(jnp.float32)
            coef[pl.ds(0, ROWS), pl.ds(0, ROWS)] = corner.astype(jnp.bfloat16)
            coef[pl.ds(0, ROWS), pl.ds(ROWS, right - ROWS)] = values[:ROWS, ROWS:].astype(jnp.bfloat16)
            coef[pl.ds(ROWS, stop - ROWS), columns] = values[ROWS:].astype(jnp.bfloat16)
        else:
            coef[rows, columns] = values.astype(jnp.bfloat16)

    def vid_back(first, stop, left, right, add=False):
        rows, columns = pl.ds(first, stop - first), pl.ds(left, right - left)
        terms = jnp.dot(coef[rows, columns], txts[columns], preferred_element_type=jnp.float32)
        vid_terms[rows] = vid_terms[rows] + terms if add else terms

    def txt_back(left, right, first, stop, add=False):
        rows, columns = pl.ds(first, stop - first), pl.ds(left, right - left)
        terms = lax.dot_general(
            coef[rows, columns], vids[rows], (((0,), (0,)), ((), ())), preferred_element_type=jnp.float32
        )
        txt_terms[columns] = txt_terms[columns] + terms if add else terms

    def hand_over(*pieces):
        for piece in pieces:
            first, rows = piece
            sib_stage[pl.ds(*piece)] = txt_terms[pl.ds(2 * first + rows, rows)].astype(jnp.bfloat16)
            terms_to_sibling(piece).start()

    def join(*pieces):
        for piece in pieces:
            first, rows = piece
            terms_to_sibling(piece).wait_recv()
            here = pl.ds(2 * first, rows)
            txt_terms[here] = txt_terms[here] + sib_landed[pl.ds(*piece)].astype(jnp.float32)

    sides = (txt, vid)
    early, middle, every = 2 * EARLY, 2 * MIDDLE, 2 * ALL

    for first, second in ((0, 8), (3, 10), (1, 9), (4, 11)):
        for side in sides:
            side.take(first)
            side.send(second)
    for side in sides:
        side.take(6)
        side.send(12, 14)
    for side in sides:
        side.take(7)
        side.send(13, 15)
    to_sibling(MATE).start()
    txt.take(2, 5)
    to_sibling(UP).start()
    to_sibling(DOWN).start()
    vid.take(2, 5)
    to_sibling(OWN).wait_recv()
    to_sibling(MATE).wait_recv()
    for first, second in ((8, 16), (10, 17)):
        for side in sides:
            side.take(first)
            side.send(second)
    coefs(0, 512, 0, 512, own=True)
    for first, second in ((9, 18), (11, 19)):
        for side in sides:
            side.take(first)
            side.send(second)
    to_sibling(FAR).start()
    to_sibling(UP).wait_recv()
    to_sibling(DOWN).wait_recv()
    coefs(0, 512, 512, 1024)
    vid_back(0, 512, 0, 1024)
    txt.take(12, 14)
    to_sibling(MATE_UP[0]).start()
    to_sibling(MATE_DOWN[0]).start()
    vid.take(12, 14)
    txt_back(0, 1024, 0, 512)
    to_sibling(FAR).wait_recv()
    coefs(512, MIDDLE, 0, 1024)
    to_sibling(MATE_UP[0]).wait_recv()
    to_sibling(MATE_DOWN[0]).wait_recv()
    coefs(0, MIDDLE, 1024, middle)
    txt.take(13, 15, 16, 17, 18, 19)
    for piece in (MATE_UP[1], MATE_DOWN[1], MATE_FAR):
        to_sibling(piece).start()
    vid.take(13, 15, 16, 17, 18, 19)

    coefs(MIDDLE, ALL, 0, middle)
    txt_back(early, middle, 0, ALL)
    hand_over(MATE_UP[0], MATE_DOWN[0])
    for piece in (MATE_UP[1], MATE_DOWN[1], MATE_FAR):
        to_sibling(piece).wait_recv()
    coefs(EARLY, ALL, middle, every)
    vid_back(EARLY, MIDDLE, 0, every)
    vid.give(4)
    vid.give(6)
    join(MATE_UP[0], MATE_DOWN[0])
    txt.give(4)
    txt.give(6)
    vid_back(FIRST, ALL, 0, every)
    for i in (0, 1, 2, 3):
        vid.give(i)
    coefs(0, EARLY, middle, every)
    txt_back(2 * FIRST, every, 0, ALL)
    hand_over(MATE_FAR)
    txt_back(middle, 2 * FIRST, 0, ALL)
    hand_over(MATE_UP[1], MATE_DOWN[1])
    join(MATE_FAR)
    for i in (0, 1, 2, 3):
        txt.give(i)
    vid_back(MIDDLE, FIRST, 0, every)
    vid.give(5)
    vid.give(7)
    join(MATE_UP[1], MATE_DOWN[1])
    txt.give(5)
    txt.give(7)
    txt_back(512, 1024, 512, ALL, add=True)
    txt_back(1024, early, 0, ALL)
    hand_over(UP, DOWN, FAR)
    vid_back(512, EARLY, 0, every)
    vid_back(0, 512, 1024, every, add=True)
    join(UP, DOWN, FAR)
    for i, other in ((10, 0), (12, 1), (11, 2), (13, 3)):
        vid.give(i, other)
    vid.give(8)
    vid.give(9)
    txt.give(10, 0)
    txt.give(12, 1)
    txt.give(8)
    txt.give(9)
    txt_back(0, 512, 512, ALL, add=True)
    hand_over(MATE, OWN)
    vid.give(14, 4, 6)
    vid.give(15, 5, 7)
    join(MATE)
    txt.give(14, 4, 6)
    txt.give(15, 5, 7)
    txt.give(11, 2)
    txt.give(13, 3)
    for i, other in ((18, 10), (16, 12), (19, 11), (17, 13)):
        for side in (vid, txt):
            side.give(i, other)

    back = scale * vid.own()
    unit = vid_unit[...]
    back = (back - unit * jnp.sum(unit * back, axis=1, keepdims=True)) / vid_norm[...]
    pool[...] = back / count_col[...]
    pool_out = pltpu.make_async_copy(pool, pool_ref, load_sems.at[2])
    pool_out.start()
    join(OWN)
    back = scale * txt.own()
    unit = txt_unit[...]
    txt_unit[...] = (back - unit * jnp.sum(unit * back, axis=1, keepdims=True)) / txt_norm[...]
    text_out = pltpu.make_async_copy(txt_unit, text_ref, load_sems.at[3])
    text_out.start()

    vid.finish()
    txt.finish()
    for piece in PIECES:
        to_sibling(piece).wait_send()
        terms_to_sibling(piece).wait_send()
    pool_out.wait()
    text_out.wait()


def spread(counts_ref, pool_hbm, text_hbm, clip_hbm, text_out, pool, text, clip, load_sems, store_sems):
    videos, slots, width = clip.shape
    parts = store_sems.shape[0] - 1
    step = videos // parts
    load_text = pltpu.make_async_copy(text_hbm, text, load_sems.at[parts])
    store_text = pltpu.make_async_copy(text, text_out, store_sems.at[parts])

    def part(i):
        return pl.ds(i * step, step)

    def load(i):
        return pltpu.make_async_copy(pool_hbm.at[part(i)], pool.at[part(i)], load_sems.at[i])

    def store(i):
        return pltpu.make_async_copy(clip.at[part(i)], clip_hbm.at[part(i)], store_sems.at[i])

    for i in range(parts):
        load(i).start()
    load_text.start()
    slot = lax.broadcasted_iota(jnp.int32, (slots, width), 0)
    for i in range(parts):
        load(i).wait()
        for video in range(i * step, (i + 1) * step):
            row = jnp.broadcast_to(pool[pl.ds(video, 1)], (slots, width))
            clip[video] = jnp.where(slot < counts_ref[video], row, 0.0)
        store(i).start()
    load_text.wait()
    store_text.start()
    for i in range(parts):
        store(i).wait()
    store_text.wait()


def on_device(clips, counts, texts, log_scale, bias):
    videos, slots, width = clips.shape
    bf16, f32 = jnp.bfloat16, jnp.float32
    smem = pl.BlockSpec(memory_space=pltpu.SMEM)
    vmem = pl.BlockSpec(memory_space=pltpu.VMEM)
    hbm = pl.BlockSpec(memory_space=pl.ANY)
    dma = pltpu.SemaphoreType.DMA
    own = jax.ShapeDtypeStruct((videos, width), f32)
    pool_grad, text_grad = pl.pallas_call(
        kernel,
        out_shape=(own, own),
        in_specs=[smem, smem, vmem, hbm, hbm],
        out_specs=(hbm, hbm),
        scratch_shapes=[
            pltpu.VMEM((ROWS, width), bf16),
            pltpu.VMEM((ROWS * SLOTS, width), bf16),
            pltpu.VMEM((BLOCKS * ROWS, width), bf16),
            pltpu.VMEM((2 * BLOCKS * ROWS, width), bf16),
            pltpu.VMEM((BLOCKS * ROWS, 2 * BLOCKS * ROWS), bf16),
            pltpu.VMEM((ROWS, width), f32),
            pltpu.VMEM((ROWS, width), f32),
            pltpu.VMEM((ROWS, 1), f32),
            pltpu.VMEM((ROWS, 1), f32),
            pltpu.VMEM((ROWS, width), f32),
            pltpu.VMEM((ROWS, 1), f32),
            pltpu.VMEM((BLOCKS * ROWS, width), f32),
            pltpu.VMEM((2 * BLOCKS * ROWS, width), f32),
            pltpu.VMEM(((BLOCKS - 1) * ROWS, width), bf16),
            pltpu.VMEM(((BLOCKS - 1) * ROWS, width), bf16),
            pltpu.VMEM(((BLOCKS - 1) * ROWS, width), bf16),
            pltpu.VMEM(((BLOCKS - 1) * ROWS, width), bf16),
            pltpu.VMEM((BLOCKS * ROWS, width), bf16),
            pltpu.VMEM((BLOCKS * ROWS, width), bf16),
            dma((4,)),
            dma((2, len(GATHER))),
            dma((2, len(REDUCE))),
            dma((2, len(GATHER))),
            dma((2, len(REDUCE))),
            dma((2, len(PIECES))),
            dma((2, len(PIECES))),
        ],
        compiler_params=pltpu.CompilerParams(
            collective_id=0, has_side_effects=True, vmem_limit_bytes=60 * 1024 * 1024
        ),
        cost_estimate=pl.CostEstimate(
            flops=6 * 1024 * 2048 * width, bytes_accessed=4 * 1024 * 1024, transcendentals=2 * 1024 * 2048
        ),
    )(log_scale, bias, counts.reshape(1, videos), texts, clips.reshape(videos * slots, width))
    return pl.pallas_call(
        spread,
        out_shape=(jax.ShapeDtypeStruct((videos, slots, width), f32), own),
        in_specs=[smem, hbm, hbm],
        out_specs=(hbm, hbm),
        scratch_shapes=[
            pltpu.VMEM((videos, width), f32),
            pltpu.VMEM((videos, width), f32),
            pltpu.VMEM((videos, slots, width), f32),
            dma((5,)),
            dma((5,)),
        ],
        compiler_params=pltpu.CompilerParams(vmem_limit_bytes=60 * 1024 * 1024),
        cost_estimate=pl.CostEstimate(flops=0, bytes_accessed=6 * 1024 * 1024, transcendentals=0),
    )(counts, pool_grad, text_grad)


def solution(mesh):
    return jax.shard_map(
        on_device,
        mesh=mesh,
        in_specs=(
            P(("group", "inner"), None, None),
            P(("group", "inner")),
            P(("group", "inner"), None),
            P(),
            P(),
        ),
        out_specs=(P(("group", "inner"), None, None), P(("group", "inner"), None)),
        check_vma=False,
    )
```

```python
import functools

import jax
import jax.numpy as jnp
from jax import lax
from jax.experimental import pallas as pl
from jax.experimental.pallas import tpu as pltpu
from jax.sharding import PartitionSpec as P

MESH = pl.DeviceIdType.MESH
ROWS = 128
SLOTS = 8
BLOCKS = 8
EPS = 1e-06

OWN, MATE, UP, DOWN, FAR = ((i * ROWS, ROWS) for i in range(5))
MATE_UP = ((640, 64), (768, 64))
MATE_DOWN = ((704, 64), (832, 64))
MATE_FAR = (896, ROWS)
PIECES = (OWN, MATE, UP, DOWN, FAR, MATE_UP[0], MATE_DOWN[0], MATE_UP[1], MATE_DOWN[1], MATE_FAR)
EARLY, MIDDLE, FIRST, ALL = 640, 768, 896, 1024


def device_at(x, y, z, core):
    return ((x % 2) * 8 + z * 2 + core, y * 2 + x // 2)


class Places:
    def __init__(self):
        group, inner = lax.axis_index("group"), lax.axis_index("inner")
        core, z, y = group % 2, (group // 2) % 4, inner // 2
        x = (inner % 2) * 2 + group // 8
        odd = x % 2
        self.sibling = device_at(x, y, z, 1 - core)
        self.vid = (
            device_at(x + 1 - 2 * odd, y, z, core),
            device_at(x, (y + 1) % 4, z, core),
            device_at(x, (y + 3) % 4, z, core),
        )
        self.txt = (
            device_at((x + 3 + 2 * odd) % 4, y, z, core),
            device_at(x, y, (z + 1) % 4, core),
            device_at(x, y, (z + 3) % 4, core),
        )

    def all(self):
        return (self.sibling, *self.vid, *self.txt)


GATHER = (
    *((1, OWN, DOWN, row, rows) for row, rows in ((0, 32), (32, 32), (64, 64))),
    *((2, OWN, UP, row, rows) for row, rows in ((64, 32), (96, 32), (0, 64))),
    *((0, OWN, MATE, row, 64) for row in (0, 64)),
    *((1, DOWN, FAR, row, 32) for row in (0, 32)),
    *((2, UP, FAR, row, 32) for row in (64, 96)),
    *((1, MATE, MATE_DOWN, row, 64) for row in (0, 64)),
    *((2, MATE, MATE_UP, row, 64) for row in (0, 64)),
    *((0, FAR, MATE_FAR, row, 32) for row in (0, 64, 32, 96)),
)
REDUCE = (
    *((0, MATE_FAR, row, 32) for row in (0, 64, 32, 96)),
    *((1, MATE_UP[half], 0, 64) for half in (0, 1)),
    *((2, MATE_DOWN[half], 0, 64) for half in (0, 1)),
    (1, UP, 0, 32),
    (2, DOWN, 64, 32),
    *((2, FAR, row, 32) for row in (0, 32)),
    *((1, FAR, row, 32) for row in (64, 96)),
    *((0, MATE, row, 64) for row in (0, 64)),
    *((1, UP, row, 32) for row in (64, 96)),
    *((2, DOWN, row, 32) for row in (0, 32)),
    (1, UP, 32, 32),
    (2, DOWN, 96, 32),
)
PLACE = tuple(sum(message[3] for message in REDUCE[:i]) for i in range(len(REDUCE)))


class Side:
    def __init__(self, cores, near, blocks, terms, stage, landed, gather_sems, reduce_sems):
        self.cores, self.near, self.blocks = cores, near, blocks
        self.terms, self.stage, self.landed = terms, stage, landed
        self.gather_sems, self.reduce_sems = gather_sems, reduce_sems

    def rows(self, piece, row, rows):
        if isinstance(piece[0], tuple):
            piece, row = piece[row // 64], row % 64
        return pl.ds(self.cores * piece[0] + row, rows)

    def gather(self, i):
        to, source, target, row, rows = GATHER[i]
        return pltpu.make_async_remote_copy(
            src_ref=self.blocks.at[self.rows(source, row, rows)],
            dst_ref=self.blocks.at[self.rows(target, row, rows)],
            send_sem=self.gather_sems.at[0, i],
            recv_sem=self.gather_sems.at[1, i],
            device_id=self.near[to],
            device_id_type=MESH,
        )

    def send(self, *ids):
        for i in ids:
            self.gather(i).start()

    def take(self, *ids):
        for i in ids:
            self.gather(i).wait_recv()

    def place(self, i):
        return pl.ds(PLACE[i], REDUCE[i][3])

    def reduce(self, i):
        here = self.place(i)
        return pltpu.make_async_remote_copy(
            src_ref=self.stage.at[here],
            dst_ref=self.landed.at[here],
            send_sem=self.reduce_sems.at[0, i],
            recv_sem=self.reduce_sems.at[1, i],
            device_id=self.near[REDUCE[i][0]],
            device_id_type=MESH,
        )

    def arrived(self, i):
        self.reduce(i).wait_recv()
        return self.landed[self.place(i)].astype(jnp.float32)

    def give(self, i, *others):
        _, piece, row, rows = REDUCE[i]
        total = self.terms[self.rows(piece, row, rows)]
        for j in others:
            total = total + self.arrived(j)
        self.stage[self.place(i)] = total.astype(jnp.bfloat16)
        self.reduce(i).start()

    def own(self):
        top = jnp.concatenate([self.arrived(8), self.arrived(20)], axis=0) + self.arrived(14)
        top = top + jnp.concatenate([self.arrived(18), self.arrived(19)], axis=0)
        bottom = jnp.concatenate([self.arrived(9), self.arrived(21)], axis=0) + self.arrived(15)
        bottom = bottom + jnp.concatenate([self.arrived(16), self.arrived(17)], axis=0)
        top = top + self.terms[self.rows(OWN, 0, 64)]
        bottom = bottom + self.terms[self.rows(OWN, 64, 64)]
        return jnp.concatenate([top, bottom], axis=0)

    def finish(self):
        for i in range(len(GATHER)):
            self.gather(i).wait_send()
        for i in range(len(REDUCE)):
            self.reduce(i).wait_send()


def kernel(
    log_scale_ref, bias_ref, counts_ref, texts_hbm, clips_hbm,
    pool_ref, text_ref,
    texts, clips, vids, txts, coef, pool,
    vid_unit, vid_norm, count_col, txt_unit, txt_norm,
    vid_terms, txt_terms, vid_stage, vid_landed, txt_stage, txt_landed, sib_stage, sib_landed,
    load_sems, vid_gather, vid_reduce, txt_gather, txt_reduce, sib_gather, sib_reduce,
):
    places = Places()
    barrier = pltpu.get_barrier_semaphore()
    for near in places.all():
        pl.semaphore_signal(barrier, inc=1, device_id=near, device_id_type=MESH)
    load_texts = pltpu.make_async_copy(texts_hbm, texts, load_sems.at[0])
    load_clips = pltpu.make_async_copy(clips_hbm, clips, load_sems.at[1])
    load_texts.start()
    load_clips.start()

    vid = Side(1, places.vid, vids, vid_terms, vid_stage, vid_landed, vid_gather, vid_reduce)
    txt = Side(2, places.txt, txts, txt_terms, txt_stage, txt_landed, txt_gather, txt_reduce)

    def to_sibling(piece):
        first, rows = piece
        return pltpu.make_async_remote_copy(
            src_ref=txts.at[pl.ds(2 * first, rows)],
            dst_ref=txts.at[pl.ds(2 * first + rows, rows)],
            send_sem=sib_gather.at[0, PIECES.index(piece)],
            recv_sem=sib_gather.at[1, PIECES.index(piece)],
            device_id=places.sibling,
            device_id_type=MESH,
        )

    def terms_to_sibling(piece):
        return pltpu.make_async_remote_copy(
            src_ref=sib_stage.at[pl.ds(*piece)],
            dst_ref=sib_landed.at[pl.ds(*piece)],
            send_sem=sib_reduce.at[0, PIECES.index(piece)],
            recv_sem=sib_reduce.at[1, PIECES.index(piece)],
            device_id=places.sibling,
            device_id_type=MESH,
        )

    scale = jnp.exp(jnp.full((1, 1), log_scale_ref[0], jnp.float32))
    bias = bias_ref[0]

    load_texts.wait()
    text_f = texts[...].astype(jnp.float32)
    norm = jnp.sqrt(jnp.sum(text_f * text_f, axis=1, keepdims=True) + EPS)
    unit = text_f / norm
    txt_unit[...] = unit
    txt_norm[...] = norm
    txts[pl.ds(0, ROWS)] = unit.astype(jnp.bfloat16)

    wide = jnp.broadcast_to(counts_ref[...].astype(jnp.float32), (ROWS, ROWS))
    column = jnp.transpose(wide)[:, 0:1]
    count_col[...] = column
    shape = (ROWS, ROWS * SLOTS)
    slot = lax.broadcasted_iota(jnp.int32, shape, 1)
    video = lax.broadcasted_iota(jnp.int32, shape, 0)
    slot = slot - video * SLOTS
    used = jnp.logical_and(slot >= 0, slot.astype(jnp.float32) < column)
    load_clips.wait()
    pooled = jnp.dot(
        used.astype(jnp.float32).astype(jnp.bfloat16), clips[...], preferred_element_type=jnp.float32
    ) / column
    norm = jnp.sqrt(jnp.sum(pooled * pooled, axis=1, keepdims=True) + EPS)
    unit = pooled / norm
    vid_unit[...] = unit
    vid_norm[...] = norm
    vids[pl.ds(0, ROWS)] = unit.astype(jnp.bfloat16)

    pl.semaphore_wait(barrier, len(places.all()))
    for side in (txt, vid):
        side.send(0, 3, 6)
    to_sibling(OWN).start()
    for side in (txt, vid):
        side.send(1, 4, 2, 5, 7)

    def coefs(first, stop, left, right, own=False):
        rows, columns = pl.ds(first, stop - first), pl.ds(left, right - left)
        dots = lax.dot_general(
            vids[rows], txts[columns], (((1,), (1,)), ((), ())), preferred_element_type=jnp.float32
        )
        logits = scale * dots + bias
        values = 1.0 / (1.0 + jnp.exp(-logits))
        if own:
            row = lax.broadcasted_iota(jnp.int32, (ROWS, ROWS), 0)
            col = lax.broadcasted_iota(jnp.int32, (ROWS, ROWS), 1)
            corner = values[:ROWS, :ROWS] - (row == col).astype(jnp.float32)
            coef[pl.ds(0, ROWS), pl.ds(0, ROWS)] = corner.astype(jnp.bfloat16)
            coef[pl.ds(0, ROWS), pl.ds(ROWS, right - ROWS)] = values[:ROWS, ROWS:].astype(jnp.bfloat16)
            coef[pl.ds(ROWS, stop - ROWS), columns] = values[ROWS:].astype(jnp.bfloat16)
        else:
            coef[rows, columns] = values.astype(jnp.bfloat16)

    def vid_back(first, stop, left, right, add=False):
        rows, columns = pl.ds(first, stop - first), pl.ds(left, right - left)
        terms = jnp.dot(coef[rows, columns], txts[columns], preferred_element_type=jnp.float32)
        vid_terms[rows] = vid_terms[rows] + terms if add else terms

    def txt_back(left, right, first, stop, add=False):
        rows, columns = pl.ds(first, stop - first), pl.ds(left, right - left)
        terms = lax.dot_general(
            coef[rows, columns], vids[rows], (((0,), (0,)), ((), ())), preferred_element_type=jnp.float32
        )
        txt_terms[columns] = txt_terms[columns] + terms if add else terms

    def hand_over(*pieces):
        for piece in pieces:
            first, rows = piece
            sib_stage[pl.ds(*piece)] = txt_terms[pl.ds(2 * first + rows, rows)].astype(jnp.bfloat16)
            terms_to_sibling(piece).start()

    def join(*pieces):
        for piece in pieces:
            first, rows = piece
            terms_to_sibling(piece).wait_recv()
            here = pl.ds(2 * first, rows)
            txt_terms[here] = txt_terms[here] + sib_landed[pl.ds(*piece)].astype(jnp.float32)

    sides = (txt, vid)
    early, middle, every = 2 * EARLY, 2 * MIDDLE, 2 * ALL

    for first, second in ((0, 8), (3, 10), (1, 9), (4, 11)):
        for side in sides:
            side.take(first)
            side.send(second)
    for side in sides:
        side.take(6)
        side.send(12, 14)
    for side in sides:
        side.take(7)
        side.send(13, 15)
    to_sibling(MATE).start()
    txt.take(2, 5)
    to_sibling(UP).start()
    to_sibling(DOWN).start()
    vid.take(2, 5)
    to_sibling(OWN).wait_recv()
    to_sibling(MATE).wait_recv()
    for first, second in ((8, 16), (10, 17)):
        for side in sides:
            side.take(first)
            side.send(second)
    coefs(0, 512, 0, 512, own=True)
    for first, second in ((9, 18), (11, 19)):
        for side in sides:
            side.take(first)
            side.send(second)
    to_sibling(FAR).start()
    to_sibling(UP).wait_recv()
    to_sibling(DOWN).wait_recv()
    coefs(0, 512, 512, 1024)
    vid_back(0, 512, 0, 1024)
    txt.take(12, 14)
    to_sibling(MATE_UP[0]).start()
    to_sibling(MATE_DOWN[0]).start()
    vid.take(12, 14)
    txt_back(0, 1024, 0, 512)
    to_sibling(FAR).wait_recv()
    coefs(512, MIDDLE, 0, 1024)
    to_sibling(MATE_UP[0]).wait_recv()
    to_sibling(MATE_DOWN[0]).wait_recv()
    coefs(0, MIDDLE, 1024, middle)
    txt.take(13, 15, 16, 17, 18, 19)
    for piece in (MATE_UP[1], MATE_DOWN[1], MATE_FAR):
        to_sibling(piece).start()
    vid.take(13, 15, 16, 17, 18, 19)

    coefs(MIDDLE, ALL, 0, middle)
    txt_back(early, middle, 0, ALL)
    hand_over(MATE_UP[0], MATE_DOWN[0])
    for piece in (MATE_UP[1], MATE_DOWN[1], MATE_FAR):
        to_sibling(piece).wait_recv()
    coefs(EARLY, ALL, middle, every)
    vid_back(EARLY, MIDDLE, 0, every)
    vid.give(4)
    vid.give(6)
    join(MATE_UP[0], MATE_DOWN[0])
    txt.give(4)
    txt.give(6)
    vid_back(FIRST, ALL, 0, every)
    for i in (0, 1, 2, 3):
        vid.give(i)
    coefs(0, EARLY, middle, every)
    txt_back(2 * FIRST, every, 0, ALL)
    hand_over(MATE_FAR)
    txt_back(middle, 2 * FIRST, 0, ALL)
    hand_over(MATE_UP[1], MATE_DOWN[1])
    join(MATE_FAR)
    for i in (0, 1, 2, 3):
        txt.give(i)
    vid_back(MIDDLE, FIRST, 0, every)
    vid.give(5)
    vid.give(7)
    join(MATE_UP[1], MATE_DOWN[1])
    txt.give(5)
    txt.give(7)
    txt_back(512, 1024, 512, ALL, add=True)
    txt_back(1024, early, 0, ALL)
    hand_over(UP, DOWN, FAR)
    vid_back(512, EARLY, 0, every)
    vid_back(0, 512, 1024, every, add=True)
    join(UP, DOWN, FAR)
    for i, other in ((10, 0), (12, 1), (11, 2), (13, 3)):
        vid.give(i, other)
    for i in (8, 9, 20, 21):
        vid.give(i)
    txt.give(10, 0)
    txt.give(12, 1)
    txt.give(8)
    txt.give(9)
    txt_back(0, 512, 512, ALL, add=True)
    hand_over(MATE, OWN)
    vid.give(14, 4, 6)
    vid.give(15, 5, 7)
    join(MATE)
    txt.give(14, 4, 6)
    txt.give(15, 5, 7)
    txt.give(11, 2)
    txt.give(13, 3)
    txt.give(20)
    txt.give(21)
    for i, other in ((18, 10), (16, 12), (19, 11), (17, 13)):
        for side in (vid, txt):
            side.give(i, other)

    back = scale * vid.own()
    unit = vid_unit[...]
    back = (back - unit * jnp.sum(unit * back, axis=1, keepdims=True)) / vid_norm[...]
    pool[...] = back / count_col[...]
    pool_out = pltpu.make_async_copy(pool, pool_ref, load_sems.at[2])
    pool_out.start()
    join(OWN)
    back = scale * txt.own()
    unit = txt_unit[...]
    txt_unit[...] = (back - unit * jnp.sum(unit * back, axis=1, keepdims=True)) / txt_norm[...]
    text_out = pltpu.make_async_copy(txt_unit, text_ref, load_sems.at[3])
    text_out.start()

    vid.finish()
    txt.finish()
    for piece in PIECES:
        to_sibling(piece).wait_send()
        terms_to_sibling(piece).wait_send()
    pool_out.wait()
    text_out.wait()


def spread(counts_ref, pool_hbm, text_hbm, clip_hbm, text_out, pool, text, clip, load_sems, store_sems):
    videos, slots, width = clip.shape
    parts = store_sems.shape[0] - 1
    step = videos // parts
    load_text = pltpu.make_async_copy(text_hbm, text, load_sems.at[parts])
    store_text = pltpu.make_async_copy(text, text_out, store_sems.at[parts])

    def part(i):
        return pl.ds(i * step, step)

    def load(i):
        return pltpu.make_async_copy(pool_hbm.at[part(i)], pool.at[part(i)], load_sems.at[i])

    def store(i):
        return pltpu.make_async_copy(clip.at[part(i)], clip_hbm.at[part(i)], store_sems.at[i])

    for i in range(parts):
        load(i).start()
    load_text.start()
    slot = lax.broadcasted_iota(jnp.int32, (slots, width), 0)
    for i in range(parts):
        load(i).wait()
        for video in range(i * step, (i + 1) * step):
            row = jnp.broadcast_to(pool[pl.ds(video, 1)], (slots, width))
            clip[video] = jnp.where(slot < counts_ref[video], row, 0.0)
        store(i).start()
    load_text.wait()
    store_text.start()
    for i in range(parts):
        store(i).wait()
    store_text.wait()


def on_device(clips, counts, texts, log_scale, bias):
    videos, slots, width = clips.shape
    bf16, f32 = jnp.bfloat16, jnp.float32
    smem = pl.BlockSpec(memory_space=pltpu.SMEM)
    vmem = pl.BlockSpec(memory_space=pltpu.VMEM)
    hbm = pl.BlockSpec(memory_space=pl.ANY)
    dma = pltpu.SemaphoreType.DMA
    own = jax.ShapeDtypeStruct((videos, width), f32)
    pool_grad, text_grad = pl.pallas_call(
        kernel,
        out_shape=(own, own),
        in_specs=[smem, smem, vmem, hbm, hbm],
        out_specs=(hbm, hbm),
        scratch_shapes=[
            pltpu.VMEM((ROWS, width), bf16),
            pltpu.VMEM((ROWS * SLOTS, width), bf16),
            pltpu.VMEM((BLOCKS * ROWS, width), bf16),
            pltpu.VMEM((2 * BLOCKS * ROWS, width), bf16),
            pltpu.VMEM((BLOCKS * ROWS, 2 * BLOCKS * ROWS), bf16),
            pltpu.VMEM((ROWS, width), f32),
            pltpu.VMEM((ROWS, width), f32),
            pltpu.VMEM((ROWS, 1), f32),
            pltpu.VMEM((ROWS, 1), f32),
            pltpu.VMEM((ROWS, width), f32),
            pltpu.VMEM((ROWS, 1), f32),
            pltpu.VMEM((BLOCKS * ROWS, width), f32),
            pltpu.VMEM((2 * BLOCKS * ROWS, width), f32),
            pltpu.VMEM(((BLOCKS - 1) * ROWS, width), bf16),
            pltpu.VMEM(((BLOCKS - 1) * ROWS, width), bf16),
            pltpu.VMEM(((BLOCKS - 1) * ROWS, width), bf16),
            pltpu.VMEM(((BLOCKS - 1) * ROWS, width), bf16),
            pltpu.VMEM((BLOCKS * ROWS, width), bf16),
            pltpu.VMEM((BLOCKS * ROWS, width), bf16),
            dma((4,)),
            dma((2, len(GATHER))),
            dma((2, len(REDUCE))),
            dma((2, len(GATHER))),
            dma((2, len(REDUCE))),
            dma((2, len(PIECES))),
            dma((2, len(PIECES))),
        ],
        compiler_params=pltpu.CompilerParams(
            collective_id=0, has_side_effects=True, vmem_limit_bytes=60 * 1024 * 1024
        ),
        cost_estimate=pl.CostEstimate(
            flops=6 * 1024 * 2048 * width, bytes_accessed=4 * 1024 * 1024, transcendentals=2 * 1024 * 2048
        ),
    )(log_scale, bias, counts.reshape(1, videos), texts, clips.reshape(videos * slots, width))
    return pl.pallas_call(
        spread,
        out_shape=(jax.ShapeDtypeStruct((videos, slots, width), f32), own),
        in_specs=[smem, hbm, hbm],
        out_specs=(hbm, hbm),
        scratch_shapes=[
            pltpu.VMEM((videos, width), f32),
            pltpu.VMEM((videos, width), f32),
            pltpu.VMEM((videos, slots, width), f32),
            dma((5,)),
            dma((5,)),
        ],
        compiler_params=pltpu.CompilerParams(vmem_limit_bytes=60 * 1024 * 1024),
        cost_estimate=pl.CostEstimate(flops=0, bytes_accessed=6 * 1024 * 1024, transcendentals=0),
    )(counts, pool_grad, text_grad)


def solution(mesh):
    return jax.shard_map(
        on_device,
        mesh=mesh,
        in_specs=(
            P(("group", "inner"), None, None),
            P(("group", "inner")),
            P(("group", "inner"), None),
            P(),
            P(),
        ),
        out_specs=(P(("group", "inner"), None, None), P(("group", "inner"), None)),
        check_vma=False,
    )
```
